32 devices in a mesh: ctx: 16 (over z, y, core), exp: 2 (over x).
Axes of the slice: x: 2, y: 2, z: 4, core: 2. Of those that a mesh axis runs over, the one named last changes fastest.
Arguments:
- ssm_input: bfloat16 [2048, 4096], P('ctx', 'exp'), may hold values from -6 to 6
- gate_input: bfloat16 [2048, 4096], P('ctx', 'exp'), may hold values from -6 to 6
- b_input: bfloat16 [2048, 1024], P('ctx', 'exp'), may hold values from -6 to 6
- c_input: bfloat16 [2048, 1024], P('ctx', 'exp'), may hold values from -6 to 6
- step_size: float32 [64, 2048], P('exp', 'ctx'), may hold values from 0.5 to 4096
- decay_rate: float32 [64], P('exp'), may hold values from 9.765625e-05 to 0.1
- norm_gain: float32 [4096], P('exp'), may hold values from 0.1 to 1.9
- out_weight: bfloat16 [4096, 2048], P('exp'), may hold values from -0.125 to 0.125
- stream: bfloat16 [2048, 2048], P('ctx', 'exp'), may hold values from -7 to 7
- moe_gain: float32 [2048], replicated, may hold values from 0.1 to 1.9
- router: bfloat16 [2048, 16], replicated, may hold values from -0.125 to 0.125
- expert_ids: int32 [2048, 6], P('ctx'), may hold values from 0 to 15, all different within a row; in each aligned block of 128 rows (0 to 127, 128 to 255, ...) at most 60 rows name the same one
- w_gate: bfloat16 [16, 1408, 2048], P('ctx', 'exp'), may hold values from -0.125 to 0.125
- w_up: bfloat16 [16, 1408, 2048], P('ctx', 'exp'), may hold values from -0.125 to 0.125
- w_down: bfloat16 [16, 1408, 2048], P('ctx', 'exp'), may hold values from -0.21875 to 0.21875
Outputs:
- layer_out: bfloat16 [2048, 2048], P('ctx', 'exp')
The draws below stay inside these ranges and needn't reach their ends.
Inputs may be any that keep to these rules, and one draw needn't show every extreme that they name: `expert_ids`: each row names 6 different experts; among the 128 rows of one device (aligned blocks of 128 rows) no expert is named by more than 60 rows, a bound that some block reaches.
All inputs are finite; a program needn't handle non-finite values.
Results may differ from the reference program's by a relative error of at most 0.024.
Values may be sent and summed in bfloat16 or wider, within the bound.
No kernel may reach another device: no remote copies, remote signals or barrier semaphores. Data moves between devices by JAX's collectives and lax.ppermute only.
A program may use at most 128 MiB of HBM per device.

```python
import math
import jax
import jax.numpy as jnp
import numpy as np
from jax import lax

D = 2048
HEADS = 64
P_SIZE = 64
N = 128
GROUPS = 8
FF = 1408
TOP = 6
TOK_DEV = 128
TOKENS = 2048
EXPERTS = 16
CAP = 60
N_CTX = 16
N_EXP = 2


def rate_table(key):
    base_key = jax.random.fold_in(key, 101)
    key_slow, key_fast, key_pick = jax.random.split(base_key, 3)
    slow_rate = jnp.exp(jax.random.uniform(key_slow, (HEADS,), jnp.float32, math.log(0.2 / TOKENS), math.log(1.0 / TOKENS)))
    fast_rate = jnp.exp(jax.random.uniform(key_fast, (HEADS,), jnp.float32, math.log(0.02), math.log(0.1)))
    keep_share = 0.5
    chosen_slow = jax.random.uniform(key_pick, (HEADS,), jnp.float32) < keep_share
    return jnp.where(chosen_slow, slow_rate, fast_rate).astype(jnp.float32)


def draw_decay_rate(key, part):
    return rate_table(key)


def draw_step_size(key, part):
    speed_numbers = rate_table(key)
    base_key = jax.random.fold_in(key, 202)
    key_base, key_place, key_loss = jax.random.split(base_key, 3)
    layer_result_tensor = jnp.exp(jax.random.uniform(key_base, (HEADS, TOKENS), jnp.float32, math.log(0.5), math.log(2.0)))
    destination_entries = jax.random.randint(key_place, (3,), 0, TOKENS)
    dropped_portion = jax.random.uniform(key_loss, (3,), jnp.float32, 0.2, 0.3)
    matrix_position = jnp.arange(TOKENS)[None, :]
    for position_number in range(3):
        jump_forward_step = -jnp.log1p(-dropped_portion[position_number]) / speed_numbers[:, None]
        layer_result_tensor = jnp.where(matrix_position == destination_entries[position_number], jnp.maximum(layer_result_tensor, jump_forward_step), layer_result_tensor)
    return layer_result_tensor.astype(jnp.float32)


def draw_stream(key, part):
    base_key = jax.random.fold_in(key, 303)
    matrix_position = jnp.arange(D, dtype=jnp.float32)[None, :]
    column_rise = jnp.exp(math.log(3.0) * matrix_position / D)
    values = jnp.clip(jax.random.normal(base_key, (TOKENS, D), jnp.float32), -3.8, 3.8) * column_rise * 0.6
    return values.astype(jnp.bfloat16)


def with_spikes(array, stream_key, source, target, shards_of, factor):
    def block_of(axis_at):
        return (jnp.arange(array.shape[axis_at]) // (array.shape[axis_at] // shards_of)).reshape((-1,) + (1,) * (array.ndim - 1 - axis_at))

    near = jax.random.permutation(stream_key, shards_of)[block_of(target)]
    second = (block_of(target) + shards_of // 2) % shards_of
    return jnp.where((block_of(source) == near) | (block_of(source) == second), factor * array, array)


def block_scale(key, extent, shards, low, largest):
    def one(position, blocks):
        heights = jax.random.uniform(jax.random.fold_in(jax.random.fold_in(key, 6), position), (blocks,), jnp.float32, low / len(shards), largest / len(shards))
        return jnp.repeat(jnp.exp(heights), extent[position] // blocks).reshape((-1,) + (1,) * (len(extent) - position - 1))

    gain = one(*shards[0])
    for cut in shards[1:]:
        gain = gain * one(*cut)
    return gain


def shared_out(key, own, number, rows, number_of, top, reach, skew):
    ranking = jax.random.permutation(key, number_of)
    crowded, ordinary = load_shares(number_of, rows * top, reach, skew, True), load_shares(number_of, rows * top, reach, skew, False)
    places = jnp.arange(number_of)

    def named(tallies, turn):
        used = int((tallies > 0).sum())
        fixed = max(1, used // 4)
        shifted = fixed + (places - fixed + turn * (used - fixed)) % max(1, number_of - fixed)
        return jnp.zeros((number_of,), jnp.int32).at[ranking[jnp.where(places < fixed, places, shifted)]].set(jnp.asarray(tallies, jnp.int32))

    tallies = jnp.where(number % 4 == 0, named(crowded, number // 4), named(ordinary, number - number // 4 - 1))
    mixed = jax.random.permutation(jax.random.fold_in(own, 3), number_of)
    source_of, receiver = mixed[0:number_of // 2 * 2:2], mixed[1:number_of // 2 * 2:2]
    margin = jnp.minimum(tallies[source_of] - 1, reach - tallies[receiver]) // 2
    margin = jnp.where((source_of == ranking[0]) | (receiver == ranking[0]) | (tallies[receiver] == 0), 0, jnp.maximum(margin, 0))
    shifted = jax.random.randint(jax.random.fold_in(own, 4), (number_of // 2,), 0, 1 << 20) % (margin + 1)
    tallies = tallies.at[source_of].add(-shifted).at[receiver].add(shifted)
    items = jnp.searchsorted(jnp.cumsum(tallies), jnp.arange(rows * top), side="right").astype(jnp.int32)
    listing = items.reshape(top, rows).T
    listing = listing[jax.random.permutation(jax.random.fold_in(own, 1), rows)]
    turn = jax.random.randint(jax.random.fold_in(own, 2), (rows, 1), 0, top)
    return jnp.take_along_axis(listing, (jnp.arange(top)[None, :] + turn) % top, axis=1)


def load_shares(number_of, total, reach, lean, full):
    portions = [(1 << 20) // math.isqrt(grade ** lean) + 1 for grade in range(1, number_of + 1)]
    largest = reach if full else min(reach, max(-(-total // number_of), total * portions[0] // sum(portions)))
    least = 1 if total - largest >= number_of - 1 else 0
    counts, surplus = [largest] + [least] * (number_of - 1), total - largest - least * (number_of - 1)
    while surplus > 0:
        movable = [i for i in range(1, number_of) if counts[i] < largest] or [i for i in range(1, number_of) if counts[i] < reach]
        pool, left = sum([portions[i] for i in movable]), surplus
        for i in movable:
            more = min(reach - counts[i], max(1, left * portions[i] // pool), surplus)
            counts[i] = counts[i] + more
            surplus = surplus - more
    return np.array(counts)


def scatter_about(key, extent, scale, most, cuts=(), kind=jnp.bfloat16):
    values = jax.random.normal(key, extent, jnp.float32) * scale
    if len(cuts) > 0:
        values = block_scale(key, extent, cuts, -0.22, 0.18) * values
    return jnp.clip(values, min=-most, max=most).astype(kind)


def gaussian_with(own_key, dims, deviation, bound, cuts, heavy, kind=jnp.bfloat16):
    entries = deviation * jax.random.normal(own_key, dims, jnp.float32)
    if cuts:
        entries = entries * block_scale(own_key, dims, cuts, -0.22, 0.18)
    return jnp.clip(with_spikes(entries, jax.random.fold_in(own_key, 3), *heavy), -bound, bound).astype(kind)


def setup_inputs(seed: int = 0) -> dict:
    seeds = jax.random.split(jax.random.key(seed), 16)
    ssm_input = scatter_about(seeds[0], (TOKENS, HEADS * P_SIZE), 1.0, 6.0, ((0, 16), (1, 2)))
    gate_input = scatter_about(seeds[1], (TOKENS, HEADS * P_SIZE), 1.0, 6.0, ((0, 16), (1, 2)))
    b_input = scatter_about(seeds[2], (TOKENS, GROUPS * N), 1.0, 6.0, ((0, 16), (1, 2)))
    c_input = scatter_about(seeds[3], (TOKENS, GROUPS * N), 1.0, 6.0, ((0, 16), (1, 2)))
    step_size = draw_step_size(jax.random.fold_in(seeds[15], 71), 0)
    decay_rate = draw_decay_rate(jax.random.fold_in(seeds[15], 71), 0)
    norm_gain = jnp.clip(1.0 + 0.18 * jax.random.normal(seeds[6], (HEADS * P_SIZE,), jnp.float32), 0.1, 1.9)
    out_weight = gaussian_with(seeds[7], (HEADS * P_SIZE, D), (HEADS * P_SIZE) ** -0.5, 0.125, ((0, 2),), (0, 1, 2, 2.0))
    stream = draw_stream(jax.random.fold_in(seeds[15], 71), 0)
    moe_gain = jnp.clip(1.0 + 0.18 * jax.random.normal(seeds[9], (D,), jnp.float32), 0.1, 1.9)
    router = scatter_about(seeds[10], (D, EXPERTS), D ** -0.5, 0.125)
    expert_ids_keys = jax.random.split(jax.random.fold_in(seeds[11], 1), TOKENS // TOK_DEV)
    expert_ids_turns = jax.random.permutation(jax.random.fold_in(seeds[11], 3), TOKENS // TOK_DEV)
    expert_ids = jax.vmap(lambda own, number: shared_out(jax.random.fold_in(seeds[11], 2), own, number, TOK_DEV, EXPERTS, TOP, CAP, 2))(expert_ids_keys, expert_ids_turns).reshape((TOKENS, TOP))
    w_gate = scatter_about(seeds[12], (EXPERTS, FF, D), D ** -0.5, 0.125, ((0, 16), (1, 2)))
    w_up = scatter_about(seeds[13], (EXPERTS, FF, D), D ** -0.5, 0.125, ((0, 16), (1, 2)))
    w_down = gaussian_with(seeds[14], (EXPERTS, FF, D), FF ** -0.5, 0.21875, ((0, 16), (1, 2)), (1, 2, 2, 2.0))
    return dict(ssm_input=ssm_input, gate_input=gate_input, b_input=b_input, c_input=c_input, step_size=step_size, decay_rate=decay_rate, norm_gain=norm_gain, out_weight=out_weight, stream=stream, moe_gain=moe_gain, router=router, expert_ids=expert_ids, w_gate=w_gate, w_up=w_up, w_down=w_down)


def ssd_block(operands):
    weighted, running, b_block, c_block = operands
    scores = jnp.einsum('tgn,sgn->gts', c_block.astype(jnp.float32), b_block.astype(jnp.float32))
    ordered = running.transpose(1, 2, 0)
    spread = ordered[:, :, :, None] - ordered[:, :, None, :]
    block_len = weighted.shape[0]
    lower_mask = jnp.arange(block_len)[:, None] >= jnp.arange(block_len)[None, :]
    decay_mat = jnp.where(lower_mask, jnp.exp(jnp.where(lower_mask, spread, 0.0)), 0.0)
    mixing = (decay_mat * scores[:, None]).astype(jnp.bfloat16)
    inner = jnp.einsum('gqts,sgqp->tgqp', mixing.astype(jnp.float32), weighted.astype(jnp.float32))
    tail_decay = jnp.exp(running[-1:] - running)
    carried = (tail_decay[..., None] * weighted).astype(jnp.bfloat16)
    block_state = jnp.einsum('tgqp,tgn->gqpn', carried.astype(jnp.float32), b_block.astype(jnp.float32))
    return (inner, block_state, jnp.exp(running[-1]))

def reference(ssm_input, gate_input, b_input, c_input, step_size, decay_rate, norm_gain, out_weight, stream, moe_gain, router, expert_ids, w_gate, w_up, w_down):
    group_heads = HEADS // GROUPS
    shaped_x = ssm_input.reshape(N_CTX, TOK_DEV, GROUPS, group_heads, P_SIZE)
    step_blocks = step_size.T.reshape(N_CTX, TOK_DEV, GROUPS, group_heads)
    weighted = (step_blocks[..., None] * shaped_x).astype(jnp.bfloat16)
    log_decay = (-step_size * decay_rate[:, None]).T.reshape(N_CTX, TOK_DEV, GROUPS, group_heads)
    running = jnp.cumsum(log_decay, axis=1)
    b_blocks = b_input.reshape(N_CTX, TOK_DEV, GROUPS, N)
    c_blocks = c_input.reshape(N_CTX, TOK_DEV, GROUPS, N)
    inner, states, block_decay = lax.map(ssd_block, (weighted, running, b_blocks, c_blocks))

    def chain_step(carry, operands):
        state_now, decay_now = operands
        return (decay_now[:, :, None, None] * carry + state_now, carry)
    final_state, entering = lax.scan(chain_step, jnp.zeros((GROUPS, group_heads, P_SIZE, N), jnp.float32), (states, block_decay))
    carried_in = jnp.einsum('btgn,bgqpn->btgqp', c_blocks.astype(jnp.float32), entering, precision=lax.Precision.HIGHEST)
    ssd_out = inner + jnp.exp(running)[..., None] * carried_in
    ssd_out = ssd_out.reshape(TOKENS, GROUPS, group_heads * P_SIZE)
    gated = ssd_out * jax.nn.silu(gate_input.astype(jnp.float32)).reshape(TOKENS, GROUPS, group_heads * P_SIZE)
    mean_sq = lax.optimization_barrier(jnp.mean(gated * gated, axis=-1, keepdims=True))
    normed = ((gated * lax.rsqrt(mean_sq + 1e-05)).reshape(TOKENS, HEADS * P_SIZE) * norm_gain).astype(jnp.bfloat16)
    mixer = jnp.dot(normed, out_weight, preferred_element_type=jnp.float32)
    hidden_state = (stream.astype(jnp.float32) + mixer).astype(jnp.bfloat16)
    hidden_f = hidden_state.astype(jnp.float32)
    mean_h = lax.optimization_barrier(jnp.mean(hidden_f * hidden_f, axis=-1, keepdims=True))
    expert_in = (hidden_f * lax.rsqrt(mean_h + 1e-06) * moe_gain).astype(jnp.bfloat16)
    logits = jnp.dot(expert_in, router, preferred_element_type=jnp.float32)
    scores = jax.nn.sigmoid(logits)
    picked = jnp.take_along_axis(scores, expert_ids, axis=1)
    gates = picked / lax.optimization_barrier(jnp.sum(picked, axis=1, keepdims=True))
    rows_all = N_CTX * CAP
    id_blocks = expert_ids.reshape(N_CTX, TOK_DEV * TOP)
    one_hot = (id_blocks[..., None] == jnp.arange(EXPERTS, dtype=jnp.int32)).astype(jnp.int32)
    slot_index = lax.optimization_barrier(jnp.sum((jnp.cumsum(one_hot, axis=1) - one_hot) * one_hot, axis=-1))
    target = id_blocks * rows_all + jnp.arange(N_CTX, dtype=jnp.int32)[:, None] * CAP + slot_index
    target = target.reshape(-1).astype(jnp.int32)
    token_of = (jnp.arange(TOKENS * TOP, dtype=jnp.int32) // TOP).astype(jnp.int32)
    table = jnp.full((EXPERTS * rows_all,), TOKENS, jnp.int32).at[target].set(token_of).reshape(EXPERTS, rows_all)
    gate_table = jnp.zeros((EXPERTS * rows_all,), jnp.float32).at[target].set(gates.reshape(-1)).reshape(EXPERTS, rows_all)
    padded = jnp.concatenate([expert_in, jnp.zeros((1, D), jnp.bfloat16)], axis=0)
    slice_units = FF // N_EXP

    def expert_step(total, operands):
        token_rows, gate_rows, gate_w, up_w, down_w = operands
        inputs = padded[token_rows]
        contract = (((1,), (1,)), ((), ()))
        gate_proj = lax.dot_general(inputs, gate_w, contract, preferred_element_type=jnp.float32)
        up_proj = lax.dot_general(inputs, up_w, contract, preferred_element_type=jnp.float32)
        active = (jax.nn.silu(gate_proj) * up_proj).astype(jnp.bfloat16)
        parts = jnp.einsum('rsf,sfd->rsd', active.reshape(rows_all, N_EXP, slice_units).astype(jnp.float32), down_w.reshape(N_EXP, slice_units, D).astype(jnp.float32)).astype(jnp.bfloat16)
        summed = lax.optimization_barrier(jnp.sum(parts.astype(jnp.float32), axis=1))
        return (total.at[token_rows].add(gate_rows[:, None] * summed), None)
    moe_sum, unused = lax.scan(expert_step, jnp.zeros((TOKENS + 1, D), jnp.float32), (table, gate_table, w_gate, w_up, w_down))
    return (hidden_f + moe_sum[:TOKENS]).astype(jnp.bfloat16)
```

```python
import functools

import jax
import jax.numpy as jnp
from jax import lax
from jax.experimental import pallas as pl
from jax.experimental.pallas import tpu as pltpu
from jax.sharding import PartitionSpec as P

P_SIZE = 64
N = 128
PLANE = 4


def move(value, partner):
    return lax.ppermute(value, "ctx", [(i, partner(i)) for i in range(lax.axis_size("ctx"))])


def prefix_states(state, log_total):
    size = lax.axis_size("ctx")
    odd = lax.axis_index("ctx") % 2 == 1
    rows, width = state.shape
    half = rows // 2
    share = rows // size
    row_log = jnp.repeat(log_total, rows // log_total.shape[0])

    def halves(array):
        return array[:half], array[half:]

    def pick(flag, first, second):
        return jnp.where(flag, second, first)

    low, high = halves(state)
    log_low, log_high = halves(row_log)
    kept, given = pick(odd, low, high), pick(odd, high, low)
    kept_log, given_log = pick(odd, log_low, log_high), pick(odd, log_high, log_low)
    got = move(given, lambda i: i ^ 1)
    got_log = move(given_log, lambda i: i ^ 1)
    first, second = pick(odd, kept, got), pick(odd, got, kept)
    first_log, second_log = pick(odd, kept_log, got_log), pick(odd, got_log, kept_log)
    pair_state = jnp.exp(second_log)[:, None] * first + second
    pair_log = (first_log + second_log).reshape(size // 2, 1, share)
    log_rows = jnp.pad(pair_log, ((0, 0), (0, 7), (0, width - share)))
    sent = jnp.concatenate([pair_state.reshape(size // 2, share, width), log_rows], axis=1)
    groups = [[i for i in range(size) if i % 2 == k] for k in range(2)]

    def exchange(array):
        return lax.all_to_all(
            array, "ctx", split_axis=0, concat_axis=0, axis_index_groups=groups, tiled=True
        )

    pairs = exchange(sent)
    decay = jnp.exp(pairs[:, share, :share])
    entering = jnp.zeros((share, width), jnp.float32)
    found = []
    for pair in range(size // 2):
        found.append(entering)
        entering = decay[pair][:, None] * entering + pairs[pair, :share]
    into_first = exchange(jnp.stack(found)).reshape(half, width)
    into_second = jnp.exp(first_log)[:, None] * into_first + first
    mine, other = pick(odd, into_first, into_second), pick(odd, into_second, into_first)
    back = move(other, lambda i: i ^ 1)
    return jnp.concatenate([pick(odd, mine, back), pick(odd, back, mine)], axis=0)


def expert_kernel(
    place, mine, other, ids, moe_gain, router, w_gate, w_up, w_down, out_mine, out_other, rows, act
):
    half = mine.shape[2]
    count = mine.shape[1]
    expert = place[0]
    own = pl.multiple_of(place[1] * half, half)
    rest = pl.multiple_of((1 - place[1]) * half, half)
    gain_own, gain_rest = moe_gain[:, pl.ds(own, half)], moe_gain[:, pl.ds(rest, half)]
    for block in range(4):
        source = mine if block < 2 else other
        left = source[2 * (block % 2)].astype(jnp.float32)
        right = source[2 * (block % 2) + 1].astype(jnp.float32)
        total = jnp.sum(left * left, axis=1, keepdims=True) + jnp.sum(
            right * right, axis=1, keepdims=True
        )
        scale = lax.rsqrt(total / (2 * half) + 1e-06)
        where = pl.ds(block * count, count)
        rows[where, pl.ds(own, half)] = (left * scale * gain_own).astype(jnp.bfloat16)
        rows[where, pl.ds(rest, half)] = (right * scale * gain_rest).astype(jnp.bfloat16)
    contract = (((1,), (1,)), ((), ()))
    score = jax.nn.sigmoid(jnp.dot(rows[...], router[...], preferred_element_type=jnp.float32))
    column = lax.broadcasted_iota(jnp.int32, score.shape, 1)
    chosen = column == ids[:, 0:1]
    for choice in range(1, ids.shape[1]):
        chosen = chosen | (column == ids[:, choice : choice + 1])
    picked = jnp.where(chosen, score, 0.0)
    gate = jnp.sum(jnp.where(column == expert, picked, 0.0), axis=1, keepdims=True) / jnp.sum(
        picked, axis=1, keepdims=True
    )
    gate_proj = lax.dot_general(
        rows[...], w_gate[...], contract, preferred_element_type=jnp.float32
    )
    up_proj = lax.dot_general(rows[...], w_up[...], contract, preferred_element_type=jnp.float32)
    act[...] = (gate_proj / (1.0 + jnp.exp(-gate_proj)) * up_proj).astype(jnp.bfloat16)
    for side, start in ((0, own), (1, rest)):
        part = jnp.dot(
            act[...], w_down[:, pl.ds(start, half)], preferred_element_type=jnp.float32
        )
        part = (part * gate).astype(jnp.bfloat16)
        for block in range(4):
            target = out_mine if block < 2 else out_other
            target[2 * (block % 2) + side] = part[block * count : (block + 1) * count]


def run_expert(place, mine, other, ids, moe_gain, router, w_gate, w_up, w_down):
    count, half = mine.shape[1:]
    units, width = w_gate.shape
    vmem = pl.BlockSpec(memory_space=pltpu.VMEM)
    return pl.pallas_call(
        expert_kernel,
        out_shape=[jax.ShapeDtypeStruct(mine.shape, jnp.bfloat16)] * 2,
        in_specs=[pl.BlockSpec(memory_space=pltpu.SMEM)] + [vmem] * 8,
        out_specs=[vmem] * 2,
        scratch_shapes=[
            pltpu.VMEM((4 * count, width), jnp.bfloat16),
            pltpu.VMEM((4 * count, units), jnp.bfloat16),
        ],
        compiler_params=pltpu.CompilerParams(vmem_limit_bytes=48 * 2**20),
        cost_estimate=pl.CostEstimate(
            flops=2 * 3 * 4 * count * width * units,
            bytes_accessed=2 * (3 * units * width + 4 * mine.size),
            transcendentals=4 * count * units,
        ),
    )(place, mine, other, ids, moe_gain, router, w_gate, w_up, w_down)


def dense_experts(hidden, expert_ids, moe_gain, router, w_gate, w_up, w_down):
    size = lax.axis_size("ctx")
    planes = size // PLANE
    here, side = lax.axis_index("ctx"), lax.axis_index("exp")
    even = here % 2 == 0
    count = hidden.shape[0]

    def flip(value, bit):
        return move(value, lambda i: i ^ bit)

    def across(value):
        return lax.ppermute(value, "exp", [(0, 1), (1, 0)])

    def diagonal(value):
        pairs = [
            (i * 2 + x, i * 2 + 1 - x if i % 2 == 0 else (i ^ 2) * 2 + x)
            for i in range(size)
            for x in range(2)
        ]
        return lax.ppermute(value, ("ctx", "exp"), pairs)

    def shift(value, planes_on):
        return move(value, lambda i: (i + PLANE * planes_on) % size)

    ids = lax.all_gather(expert_ids, "ctx")
    order = jnp.stack(
        [
            (here // PLANE + plane) % planes * PLANE + ((here % PLANE) ^ flips)
            for plane in range(planes)
            for flips in (0, 2, 1, 3)
        ]
    )
    ids = ids[order].reshape(planes, PLANE * count, expert_ids.shape[1])
    place = jnp.stack([here, side]).astype(jnp.int32)
    blocks = [hidden] + [shift(hidden, -plane) for plane in range(1, planes)]
    total = hidden.astype(jnp.float32)
    for plane in range(planes):
        own = blocks[plane]
        by_y, by_x = flip(own, 2), across(own)
        by_both = diagonal(jnp.where(even, by_y, by_x))
        mine = jnp.stack([own, by_x, by_y, by_both])
        other = flip(mine, 1)
        out_mine, out_other = run_expert(
            place, mine, other, ids[plane], moe_gain[None], router, w_gate, w_up, w_down
        )
        part = (out_mine.astype(jnp.float32) + flip(out_other, 1).astype(jnp.float32)).astype(
            jnp.bfloat16
        )
        turned = diagonal(part[3])
        zero = jnp.zeros_like(turned)
        to_y = part[2] + jnp.where(even, turned, zero)
        to_x = part[1] + jnp.where(even, zero, turned)
        summed = (
            part[0].astype(jnp.float32)
            + flip(to_y, 2).astype(jnp.float32)
            + across(to_x).astype(jnp.float32)
        )
        if plane > 0:
            summed = shift(summed.astype(jnp.bfloat16), plane).astype(jnp.float32)
        total = total + summed
    return total.astype(jnp.bfloat16)


def run_rows(pieces, w_gate, w_up, w_down):
    row_count = pieces.shape[0] * pieces.shape[1]
    flattened = pieces.reshape(row_count, pieces.shape[2])
    contract = (((1,), (1,)), ((), ()))
    gate_proj = lax.dot_general(flattened, w_gate[0], contract, preferred_element_type=jnp.float32)
    up_proj = lax.dot_general(flattened, w_up[0], contract, preferred_element_type=jnp.float32)
    active = (jax.nn.silu(gate_proj) * up_proj).astype(jnp.bfloat16)
    partial_value = jnp.dot(active, w_down[0], preferred_element_type=jnp.float32).astype(
        jnp.bfloat16
    )
    full_width = partial_value.shape[1]
    shaped = partial_value.reshape(pieces.shape[0], pieces.shape[1], full_width)
    return lax.all_to_all(shaped, "ctx", split_axis=0, concat_axis=0, tiled=True)


def per_device(
    ssm_input,
    gate_input,
    b_input,
    c_input,
    step_size,
    decay_rate,
    norm_gain,
    out_weight,
    stream,
    moe_gain,
    router,
    expert_ids,
    w_gate,
    w_up,
    w_down,
):
    token_count = ssm_input.shape[0]
    head_count = step_size.shape[0]
    group_count = b_input.shape[1] // N
    per_group = head_count // group_count
    log_decay = -step_size * decay_rate[:, None]
    running = jnp.cumsum(log_decay, axis=1).T.reshape(token_count, group_count, per_group)
    shaped_x = ssm_input.reshape(token_count, group_count, per_group, P_SIZE)
    step_rows = step_size.T.reshape(token_count, group_count, per_group)
    weighted = (step_rows[..., None] * shaped_x).astype(jnp.bfloat16)
    b_block = b_input.reshape(token_count, group_count, N)
    c_block = c_input.reshape(token_count, group_count, N)
    scores = jnp.einsum("tgn,sgn->gts", c_block, b_block, preferred_element_type=jnp.float32)
    ordered = running.transpose(1, 2, 0)
    spread = ordered[:, :, :, None] - ordered[:, :, None, :]
    lower_mask = jnp.arange(token_count)[:, None] >= jnp.arange(token_count)[None, :]
    decay_mat = jnp.where(lower_mask, jnp.exp(jnp.where(lower_mask, spread, 0.0)), 0.0)
    mixing = (decay_mat * scores[:, None]).astype(jnp.bfloat16)
    inner = jnp.einsum("gqts,sgqp->tgqp", mixing, weighted, preferred_element_type=jnp.float32)
    tail_decay = jnp.exp(running[-1:] - running)
    carried = (tail_decay[..., None] * weighted).astype(jnp.bfloat16)
    block_state = jnp.einsum("tgqp,tgn->gqpn", carried, b_block, preferred_element_type=jnp.float32)
    entering = prefix_states(
        block_state.reshape(head_count * P_SIZE, N), running[-1].reshape(head_count)
    ).reshape(group_count, per_group, P_SIZE, N)
    carried_in = jnp.einsum(
        "tgn,gqpn->tgqp", c_block.astype(jnp.float32), entering, precision=lax.Precision.HIGHEST
    )
    ssd_out = (inner + jnp.exp(running)[..., None] * carried_in).reshape(
        token_count, group_count, per_group * P_SIZE
    )
    gated = ssd_out * jax.nn.silu(gate_input.astype(jnp.float32)).reshape(
        token_count, group_count, per_group * P_SIZE
    )
    mean_sq = jnp.mean(gated * gated, axis=-1, keepdims=True)
    normed = (
        (gated * lax.rsqrt(mean_sq + 1e-05)).reshape(token_count, head_count * P_SIZE) * norm_gain
    ).astype(jnp.bfloat16)
    mixer = jnp.dot(normed, out_weight, preferred_element_type=jnp.float32)
    slice_width = stream.shape[1]
    start_col = lax.axis_index("exp") * slice_width
    expert_count = router.shape[1]
    top_count = expert_ids.shape[1]
    capacity = max(
        2, token_count * top_count // expert_count + token_count * top_count // (4 * expert_count)
    )
    exp_size = lax.axis_size("exp")
    hidden_own = lax.dynamic_slice_in_dim(mixer, start_col, slice_width, 1) + stream.astype(
        jnp.float32
    )
    for step in range(1, exp_size):
        ring = [(i, (i + step) % exp_size) for i in range(exp_size)]
        target_col = (lax.axis_index("exp") + step) % exp_size * slice_width
        theirs = lax.dynamic_slice_in_dim(mixer, target_col, slice_width, 1).astype(jnp.bfloat16)
        hidden_own = hidden_own + lax.ppermute(theirs, "exp", ring).astype(jnp.float32)
    hidden_own = hidden_own.astype(jnp.bfloat16)
    every_token = token_count * lax.axis_size("ctx")
    if exp_size == 2 and every_token <= 3 * expert_count * capacity:
        return dense_experts(
            hidden_own, expert_ids, moe_gain, router, w_gate[0], w_up[0], w_down[0]
        )
    hidden_all = lax.all_gather(hidden_own, "exp", axis=1, tiled=True)
    hidden_f = hidden_all.astype(jnp.float32)
    mean_h = jnp.mean(hidden_f * hidden_f, axis=1, keepdims=True)
    sent_rows = (hidden_f * lax.rsqrt(mean_h + 1e-06) * moe_gain).astype(jnp.bfloat16)
    logits = jnp.dot(sent_rows, router, preferred_element_type=jnp.float32)
    sigmoid_score = jax.nn.sigmoid(logits)
    expert_range = jnp.arange(expert_count, dtype=jnp.int32)
    matches = expert_ids[:, :, None] == expert_range
    picked = jnp.sum(jnp.where(matches, sigmoid_score[:, None, :], 0.0), axis=2)
    gates = picked / jnp.sum(picked, axis=1, keepdims=True)
    flat_ids = expert_ids.reshape(-1)
    one_hot = (flat_ids[:, None] == expert_range).astype(jnp.int32)
    slot_index = jnp.sum((jnp.cumsum(one_hot, axis=0) - one_hot) * one_hot, axis=1)
    target = flat_ids * capacity + slot_index
    token_of = jnp.arange(token_count * top_count, dtype=jnp.int32) // top_count
    source_row = (
        jnp.full((expert_count * capacity,), token_count, jnp.int32).at[target].set(token_of)
    )
    padded = jnp.concatenate([sent_rows, jnp.zeros((1, sent_rows.shape[1]), jnp.bfloat16)], axis=0)
    outgoing = padded[source_row].reshape(expert_count, capacity, sent_rows.shape[1])
    returned = run_rows(
        lax.all_to_all(outgoing, "ctx", split_axis=0, concat_axis=0, tiled=True),
        w_gate,
        w_up,
        w_down,
    )
    back_width = returned.shape[2]
    flat_back = returned.reshape(expert_count * capacity, back_width)
    slot_rows = target.reshape(token_count, top_count)
    moe_part = jnp.zeros((token_count, back_width), jnp.float32)
    for choice_number in range(top_count):
        picked_rows = flat_back[slot_rows[:, choice_number]].astype(jnp.float32)
        moe_part = moe_part + gates[:, choice_number][:, None] * picked_rows
    moe_sum = lax.psum_scatter(
        moe_part.astype(jnp.bfloat16), "exp", scatter_dimension=1, tiled=True
    ).astype(jnp.float32)
    return (hidden_own.astype(jnp.float32) + moe_sum).astype(jnp.bfloat16)


def solution(mesh):
    in_specs = (
        P("ctx", "exp"),
        P("ctx", "exp"),
        P("ctx", "exp"),
        P("ctx", "exp"),
        P("exp", "ctx"),
        P("exp"),
        P("exp"),
        P("exp", None),
        P("ctx", "exp"),
        P(),
        P(),
        P("ctx", None),
        P("ctx", "exp", None),
        P("ctx", "exp", None),
        P("ctx", "exp", None),
    )
    out_specs = P("ctx", "exp")
    return jax.shard_map(
        per_device, mesh=mesh, in_specs=in_specs, out_specs=out_specs, check_vma=False
    )
```

```python
import functools

import jax
import jax.numpy as jnp
from jax import lax
from jax.experimental import pallas as pl
from jax.experimental.pallas import tpu as pltpu
from jax.sharding import PartitionSpec as P

P_SIZE = 64
N = 128
PLANE = 4


def move(value, partner):
    return lax.ppermute(value, "ctx", [(i, partner(i)) for i in range(lax.axis_size("ctx"))])


def as_rows(flat, width):
    tile = 8 * width
    return jnp.pad(flat, (0, -flat.shape[0] % tile)).reshape(-1, width)


def chain_kernel(pairs, out):
    count, share, width = out.shape
    line = lax.broadcasted_iota(jnp.int32, (share, width), 0)
    lane = lax.broadcasted_iota(jnp.int32, (share, width), 1)
    entering = jnp.zeros((share, width), jnp.float32)
    for pair in range(count):
        out[pair] = entering
        logs = jnp.where(line == lane, pairs[pair, share : share + 1, :], 0.0)
        decay = jnp.exp(jnp.sum(logs, axis=1, keepdims=True))
        entering = decay * entering + pairs[pair, :share]


def prefix_states(state, log_total, extra):
    size = lax.axis_size("ctx")
    odd = lax.axis_index("ctx") % 2 == 1
    rows, width = state.shape
    half = rows // 2
    share = rows // size
    extra_rows = extra.shape[0]
    row_log = jnp.repeat(log_total, rows // log_total.shape[0])

    def halves(array):
        return array[:half], array[half:]

    def pick(flag, first, second):
        return jnp.where(flag, second, first)

    low, high = halves(state)
    log_low, log_high = halves(row_log)
    kept, given = pick(odd, low, high), pick(odd, high, low)
    kept_log, given_log = pick(odd, log_low, log_high), pick(odd, log_high, log_low)
    log_rows = as_rows(given_log, width)
    got = move(jnp.concatenate([given, log_rows, extra], axis=0), lambda i: i ^ 1)
    got_log = got[half : half + log_rows.shape[0]].reshape(-1)[:half]
    got_extra = got[half + log_rows.shape[0] :]
    got = got[:half]
    first, second = pick(odd, kept, got), pick(odd, got, kept)
    first_log, second_log = pick(odd, kept_log, got_log), pick(odd, got_log, kept_log)
    pair_extra = jnp.concatenate([pick(odd, extra, got_extra), pick(odd, got_extra, extra)], axis=0)
    pair_state = jnp.exp(second_log)[:, None] * first + second
    pair_log = (first_log + second_log).reshape(size // 2, 1, share)
    pair_log = jnp.pad(pair_log, ((0, 0), (0, 7), (0, width - share)))
    pair_extra = jnp.broadcast_to(pair_extra[None], (size // 2, 2 * extra_rows, width))
    sent = jnp.concatenate(
        [pair_state.reshape(size // 2, share, width), pair_log, pair_extra], axis=1
    )
    groups = [[i for i in range(size) if i % 2 == k] for k in range(2)]

    def exchange(array):
        return lax.all_to_all(
            array, "ctx", split_axis=0, concat_axis=0, axis_index_groups=groups, tiled=True
        )

    pairs = exchange(sent)
    found = pl.pallas_call(
        chain_kernel, out_shape=jax.ShapeDtypeStruct((size // 2, share, width), jnp.float32)
    )(pairs)
    into_first = exchange(found).reshape(half, width)
    into_second = jnp.exp(first_log)[:, None] * into_first + first
    mine, other = pick(odd, into_first, into_second), pick(odd, into_second, into_first)
    back = move(other, lambda i: i ^ 1)
    entering = jnp.concatenate([pick(odd, mine, back), pick(odd, back, mine)], axis=0)
    return entering, pairs[:, share + 8 :].reshape(size, extra_rows, width)


def expert_kernel(
    place, mine, other, ids, moe_gain, router, gate_hbm, up_hbm, down_hbm, *others
):
    out_mine, out_other, rows, act, w_gate, w_up, w_down, arrived = others[-8:]
    loads = [
        pltpu.make_async_copy(source, target, arrived.at[i])
        for i, (source, target) in enumerate(
            ((gate_hbm, w_gate), (up_hbm, w_up), (down_hbm, w_down))
        )
    ]
    for load in loads:
        load.start()
    half = mine.shape[2]
    count = mine.shape[1]
    expert = place[0]
    own = pl.multiple_of(place[1] * half, half)
    rest = pl.multiple_of((1 - place[1]) * half, half)
    gain_own, gain_rest = moe_gain[:, pl.ds(own, half)], moe_gain[:, pl.ds(rest, half)]
    for block in range(4):
        source = mine if block < 2 else other
        left = source[2 * (block % 2)].astype(jnp.float32)
        right = source[2 * (block % 2) + 1].astype(jnp.float32)
        total = jnp.sum(left * left, axis=1, keepdims=True) + jnp.sum(
            right * right, axis=1, keepdims=True
        )
        scale = lax.rsqrt(total / (2 * half) + 1e-06)
        where = pl.ds(block * count, count)
        rows[where, pl.ds(own, half)] = (left * scale * gain_own).astype(jnp.bfloat16)
        rows[where, pl.ds(rest, half)] = (right * scale * gain_rest).astype(jnp.bfloat16)
    contract = (((1,), (1,)), ((), ()))
    score = jax.nn.sigmoid(jnp.dot(rows[...], router[...], preferred_element_type=jnp.float32))
    column = lax.broadcasted_iota(jnp.int32, score.shape, 1)
    chosen = column == ids[:, 0:1]
    for choice in range(1, ids.shape[1]):
        chosen = chosen | (column == ids[:, choice : choice + 1])
    picked = jnp.where(chosen, score, 0.0)
    gate = jnp.sum(jnp.where(column == expert, picked, 0.0), axis=1, keepdims=True) / jnp.sum(
        picked, axis=1, keepdims=True
    )
    loads[0].wait()
    gate_proj = lax.dot_general(
        rows[...], w_gate[...], contract, preferred_element_type=jnp.float32
    )
    loads[1].wait()
    up_proj = lax.dot_general(rows[...], w_up[...], contract, preferred_element_type=jnp.float32)
    act[...] = (gate_proj / (1.0 + jnp.exp(-gate_proj)) * up_proj).astype(jnp.bfloat16)
    loads[2].wait()
    for side, start in ((0, own), (1, rest)):
        part = jnp.dot(
            act[...], w_down[:, pl.ds(start, half)], preferred_element_type=jnp.float32
        )
        part = (part * gate).astype(jnp.bfloat16)
        for block in range(4):
            target = out_mine if block < 2 else out_other
            target[2 * (block % 2) + side] = part[block * count : (block + 1) * count]


def run_expert(place, mine, other, ids, moe_gain, router, weights, before):
    count, half = mine.shape[1:]
    units, width = weights[0].shape
    vmem = pl.BlockSpec(memory_space=pltpu.VMEM)
    anywhere = pl.BlockSpec(memory_space=pl.ANY)
    return pl.pallas_call(
        expert_kernel,
        out_shape=[jax.ShapeDtypeStruct(mine.shape, jnp.bfloat16)] * 2,
        in_specs=[pl.BlockSpec(memory_space=pltpu.SMEM)]
        + [vmem] * 5
        + [anywhere] * (3 + len(before)),
        out_specs=[vmem] * 2,
        scratch_shapes=[
            pltpu.VMEM((4 * count, width), jnp.bfloat16),
            pltpu.VMEM((4 * count, units), jnp.bfloat16),
        ]
        + [pltpu.VMEM((units, width), jnp.bfloat16)] * 3
        + [pltpu.SemaphoreType.DMA((3,))],
        compiler_params=pltpu.CompilerParams(vmem_limit_bytes=40 * 2**20),
        cost_estimate=pl.CostEstimate(
            flops=2 * 3 * 4 * count * width * units,
            bytes_accessed=2 * (3 * units * width + 4 * mine.size),
            transcendentals=4 * count * units,
        ),
    )(place, mine, other, ids, moe_gain, router, *weights, *before)


def dense_experts(hidden, expert_ids, moe_gain, router, w_gate, w_up, w_down):
    size = lax.axis_size("ctx")
    planes = size // PLANE
    here, side = lax.axis_index("ctx"), lax.axis_index("exp")
    even = here % 2 == 0
    count = hidden.shape[0]

    def flip(value, bit):
        return move(value, lambda i: i ^ bit)

    def across(value):
        return lax.ppermute(value, "exp", [(0, 1), (1, 0)])

    def diagonal(value):
        pairs = [
            (i * 2 + x, i * 2 + 1 - x if i % 2 == 0 else (i ^ 2) * 2 + x)
            for i in range(size)
            for x in range(2)
        ]
        return lax.ppermute(value, ("ctx", "exp"), pairs)

    def shift(value, planes_on):
        return move(value, lambda i: (i + PLANE * planes_on) % size)

    order = jnp.stack(
        [
            (here // PLANE + plane) % planes * PLANE + ((here % PLANE) ^ flips)
            for plane in range(planes)
            for flips in (0, 2, 1, 3)
        ]
    )
    ids = expert_ids[order].reshape(planes, PLANE * count, expert_ids.shape[2])
    place = jnp.stack([here, side]).astype(jnp.int32)
    blocks = [hidden] + [shift(hidden, -plane) for plane in range(1, planes)]
    gathered = []
    for own in blocks:
        by_y, by_x = flip(own, 2), across(own)
        turning = jnp.where(even, by_y, by_x)
        gathered.append((own, by_x, by_y, turning))
    total = hidden.astype(jnp.float32)
    parts, turned_parts, sums = [], [], []
    weights = (w_gate, w_up, w_down)
    for plane in range(planes):
        own, by_x, by_y, turning = gathered[plane]
        mine = jnp.stack([own, by_x, by_y, diagonal(turning)])
        other = flip(mine, 1)
        before = []
        if plane + 1 < planes:
            before.append(gathered[plane + 1][3])
        if plane >= 1:
            before.append(parts[plane - 1])
        if plane >= 2:
            before.extend(turned_parts[plane - 2])
        if plane >= 3:
            before.append(sums[plane - 3])
        out_mine, out_other = run_expert(
            place, mine, other, ids[plane], moe_gain[None], router, weights, before
        )
        part = (out_mine.astype(jnp.float32) + flip(out_other, 1).astype(jnp.float32)).astype(
            jnp.bfloat16
        )
        turned = diagonal(part[3])
        zero = jnp.zeros_like(turned)
        to_y = part[2] + jnp.where(even, turned, zero)
        to_x = part[1] + jnp.where(even, zero, turned)
        summed = (
            part[0].astype(jnp.float32)
            + flip(to_y, 2).astype(jnp.float32)
            + across(to_x).astype(jnp.float32)
        )
        parts.append(part)
        turned_parts.append((to_y, to_x))
        if plane > 0:
            summed = summed.astype(jnp.bfloat16)
            sums.append(summed)
            summed = shift(summed, plane).astype(jnp.float32)
        else:
            sums.append(summed)
        total = total + summed
    return total.astype(jnp.bfloat16)


def run_rows(pieces, w_gate, w_up, w_down):
    row_count = pieces.shape[0] * pieces.shape[1]
    flattened = pieces.reshape(row_count, pieces.shape[2])
    contract = (((1,), (1,)), ((), ()))
    gate_proj = lax.dot_general(flattened, w_gate[0], contract, preferred_element_type=jnp.float32)
    up_proj = lax.dot_general(flattened, w_up[0], contract, preferred_element_type=jnp.float32)
    active = (jax.nn.silu(gate_proj) * up_proj).astype(jnp.bfloat16)
    partial_value = jnp.dot(active, w_down[0], preferred_element_type=jnp.float32).astype(
        jnp.bfloat16
    )
    full_width = partial_value.shape[1]
    shaped = partial_value.reshape(pieces.shape[0], pieces.shape[1], full_width)
    return lax.all_to_all(shaped, "ctx", split_axis=0, concat_axis=0, tiled=True)


def per_device(
    ssm_input,
    gate_input,
    b_input,
    c_input,
    step_size,
    decay_rate,
    norm_gain,
    out_weight,
    stream,
    moe_gain,
    router,
    expert_ids,
    w_gate,
    w_up,
    w_down,
):
    token_count = ssm_input.shape[0]
    head_count = step_size.shape[0]
    group_count = b_input.shape[1] // N
    per_group = head_count // group_count
    log_decay = -step_size * decay_rate[:, None]
    running = jnp.cumsum(log_decay, axis=1).T.reshape(token_count, group_count, per_group)
    shaped_x = ssm_input.reshape(token_count, group_count, per_group, P_SIZE)
    step_rows = step_size.T.reshape(token_count, group_count, per_group)
    weighted = (step_rows[..., None] * shaped_x).astype(jnp.bfloat16)
    b_block = b_input.reshape(token_count, group_count, N)
    c_block = c_input.reshape(token_count, group_count, N)
    scores = jnp.einsum("tgn,sgn->gts", c_block, b_block, preferred_element_type=jnp.float32)
    ordered = running.transpose(1, 2, 0)
    spread = ordered[:, :, :, None] - ordered[:, :, None, :]
    lower_mask = jnp.arange(token_count)[:, None] >= jnp.arange(token_count)[None, :]
    decay_mat = jnp.where(lower_mask, jnp.exp(jnp.where(lower_mask, spread, 0.0)), 0.0)
    mixing = (decay_mat * scores[:, None]).astype(jnp.bfloat16)
    inner = jnp.einsum("gqts,sgqp->tgqp", mixing, weighted, preferred_element_type=jnp.float32)
    tail_decay = jnp.exp(running[-1:] - running)
    carried = (tail_decay[..., None] * weighted).astype(jnp.bfloat16)
    block_state = jnp.einsum("tgqp,tgn->gqpn", carried, b_block, preferred_element_type=jnp.float32)
    id_rows = as_rows(expert_ids.astype(jnp.float32).reshape(-1), N)
    entering, every_ids = prefix_states(
        block_state.reshape(head_count * P_SIZE, N), running[-1].reshape(head_count), id_rows
    )
    entering = entering.reshape(group_count, per_group, P_SIZE, N)
    carried_in = jnp.einsum(
        "tgn,gqpn->tgqp", c_block.astype(jnp.float32), entering, precision=lax.Precision.HIGHEST
    )
    ssd_out = (inner + jnp.exp(running)[..., None] * carried_in).reshape(
        token_count, group_count, per_group * P_SIZE
    )
    gated = ssd_out * jax.nn.silu(gate_input.astype(jnp.float32)).reshape(
        token_count, group_count, per_group * P_SIZE
    )
    mean_sq = jnp.mean(gated * gated, axis=-1, keepdims=True)
    normed = (
        (gated * lax.rsqrt(mean_sq + 1e-05)).reshape(token_count, head_count * P_SIZE) * norm_gain
    ).astype(jnp.bfloat16)
    mixer = jnp.dot(normed, out_weight, preferred_element_type=jnp.float32)
    slice_width = stream.shape[1]
    start_col = lax.axis_index("exp") * slice_width
    expert_count = router.shape[1]
    top_count = expert_ids.shape[1]
    capacity = max(
        2, token_count * top_count // expert_count + token_count * top_count // (4 * expert_count)
    )
    exp_size = lax.axis_size("exp")
    hidden_own = lax.dynamic_slice_in_dim(mixer, start_col, slice_width, 1) + stream.astype(
        jnp.float32
    )
    for step in range(1, exp_size):
        ring = [(i, (i + step) % exp_size) for i in range(exp_size)]
        target_col = (lax.axis_index("exp") + step) % exp_size * slice_width
        theirs = lax.dynamic_slice_in_dim(mixer, target_col, slice_width, 1).astype(jnp.bfloat16)
        hidden_own = hidden_own + lax.ppermute(theirs, "exp", ring).astype(jnp.float32)
    hidden_own = hidden_own.astype(jnp.bfloat16)
    every_token = token_count * lax.axis_size("ctx")
    if exp_size == 2 and every_token <= 3 * expert_count * capacity:
        every_ids = every_ids.reshape(lax.axis_size("ctx"), -1)[:, : expert_ids.size]
        every_ids = every_ids.astype(jnp.int32).reshape(-1, *expert_ids.shape)
        return dense_experts(
            hidden_own, every_ids, moe_gain, router, w_gate[0], w_up[0], w_down[0]
        )
    hidden_all = lax.all_gather(hidden_own, "exp", axis=1, tiled=True)
    hidden_f = hidden_all.astype(jnp.float32)
    mean_h = jnp.mean(hidden_f * hidden_f, axis=1, keepdims=True)
    sent_rows = (hidden_f * lax.rsqrt(mean_h + 1e-06) * moe_gain).astype(jnp.bfloat16)
    logits = jnp.dot(sent_rows, router, preferred_element_type=jnp.float32)
    sigmoid_score = jax.nn.sigmoid(logits)
    expert_range = jnp.arange(expert_count, dtype=jnp.int32)
    matches = expert_ids[:, :, None] == expert_range
    picked = jnp.sum(jnp.where(matches, sigmoid_score[:, None, :], 0.0), axis=2)
    gates = picked / jnp.sum(picked, axis=1, keepdims=True)
    flat_ids = expert_ids.reshape(-1)
    one_hot = (flat_ids[:, None] == expert_range).astype(jnp.int32)
    slot_index = jnp.sum((jnp.cumsum(one_hot, axis=0) - one_hot) * one_hot, axis=1)
    target = flat_ids * capacity + slot_index
    token_of = jnp.arange(token_count * top_count, dtype=jnp.int32) // top_count
    source_row = (
        jnp.full((expert_count * capacity,), token_count, jnp.int32).at[target].set(token_of)
    )
    padded = jnp.concatenate([sent_rows, jnp.zeros((1, sent_rows.shape[1]), jnp.bfloat16)], axis=0)
    outgoing = padded[source_row].reshape(expert_count, capacity, sent_rows.shape[1])
    returned = run_rows(
        lax.all_to_all(outgoing, "ctx", split_axis=0, concat_axis=0, tiled=True),
        w_gate,
        w_up,
        w_down,
    )
    back_width = returned.shape[2]
    flat_back = returned.reshape(expert_count * capacity, back_width)
    slot_rows = target.reshape(token_count, top_count)
    moe_part = jnp.zeros((token_count, back_width), jnp.float32)
    for choice_number in range(top_count):
        picked_rows = flat_back[slot_rows[:, choice_number]].astype(jnp.float32)
        moe_part = moe_part + gates[:, choice_number][:, None] * picked_rows
    moe_sum = lax.psum_scatter(
        moe_part.astype(jnp.bfloat16), "exp", scatter_dimension=1, tiled=True
    ).astype(jnp.float32)
    return (hidden_own.astype(jnp.float32) + moe_sum).astype(jnp.bfloat16)


def solution(mesh):
    in_specs = (
        P("ctx", "exp"),
        P("ctx", "exp"),
        P("ctx", "exp"),
        P("ctx", "exp"),
        P("exp", "ctx"),
        P("exp"),
        P("exp"),
        P("exp", None),
        P("ctx", "exp"),
        P(),
        P(),
        P("ctx", None),
        P("ctx", "exp", None),
        P("ctx", "exp", None),
        P("ctx", "exp", None),
    )
    out_specs = P("ctx", "exp")
    return jax.shard_map(
        per_device, mesh=mesh, in_specs=in_specs, out_specs=out_specs, check_vma=False
    )
```

```python
import functools

import jax
import jax.numpy as jnp
from jax import lax
from jax.experimental import pallas as pl
from jax.experimental.pallas import tpu as pltpu
from jax.sharding import PartitionSpec as P

P_SIZE = 64
N = 128
PLANE = 4


def move(value, partner):
    return lax.ppermute(value, "ctx", [(i, partner(i)) for i in range(lax.axis_size("ctx"))])


def as_rows(flat, width):
    tile = 8 * width
    return jnp.pad(flat, (0, -flat.shape[0] % tile)).reshape(-1, width)


def chain_kernel(pairs, out):
    count, share, width = out.shape
    line = lax.broadcasted_iota(jnp.int32, (share, width), 0)
    lane = lax.broadcasted_iota(jnp.int32, (share, width), 1)
    entering = jnp.zeros((share, width), jnp.float32)
    for pair in range(count):
        out[pair] = entering
        logs = jnp.where(line == lane, pairs[pair, share : share + 1, :], 0.0)
        decay = jnp.exp(jnp.sum(logs, axis=1, keepdims=True))
        entering = decay * entering + pairs[pair, :share]


def prefix_states(state, log_total, extra):
    size = lax.axis_size("ctx")
    odd = lax.axis_index("ctx") % 2 == 1
    rows, width = state.shape
    half = rows // 2
    share = rows // size
    extra_rows = extra.shape[0]
    row_log = jnp.repeat(log_total, rows // log_total.shape[0])

    def halves(array):
        return array[:half], array[half:]

    def pick(flag, first, second):
        return jnp.where(flag, second, first)

    low, high = halves(state)
    log_low, log_high = halves(row_log)
    kept, given = pick(odd, low, high), pick(odd, high, low)
    kept_log, given_log = pick(odd, log_low, log_high), pick(odd, log_high, log_low)
    log_rows = as_rows(given_log, width)
    got = move(jnp.concatenate([given, log_rows, extra], axis=0), lambda i: i ^ 1)
    got_log = got[half : half + log_rows.shape[0]].reshape(-1)[:half]
    got_extra = got[half + log_rows.shape[0] :]
    got = got[:half]
    first, second = pick(odd, kept, got), pick(odd, got, kept)
    first_log, second_log = pick(odd, kept_log, got_log), pick(odd, got_log, kept_log)
    pair_extra = jnp.concatenate([pick(odd, extra, got_extra), pick(odd, got_extra, extra)], axis=0)
    pair_state = jnp.exp(second_log)[:, None] * first + second
    pair_log = (first_log + second_log).reshape(size // 2, 1, share)
    pair_log = jnp.pad(pair_log, ((0, 0), (0, 7), (0, width - share)))
    pair_extra = jnp.broadcast_to(pair_extra[None], (size // 2, 2 * extra_rows, width))
    sent = jnp.concatenate(
        [pair_state.reshape(size // 2, share, width), pair_log, pair_extra], axis=1
    )
    groups = [[i for i in range(size) if i % 2 == k] for k in range(2)]

    def exchange(array):
        return lax.all_to_all(
            array, "ctx", split_axis=0, concat_axis=0, axis_index_groups=groups, tiled=True
        )

    pairs = exchange(sent)
    found = pl.pallas_call(
        chain_kernel, out_shape=jax.ShapeDtypeStruct((size // 2, share, width), jnp.float32)
    )(pairs)
    into_first = exchange(found).reshape(half, width)
    into_second = jnp.exp(first_log)[:, None] * into_first + first
    mine, other = pick(odd, into_first, into_second), pick(odd, into_second, into_first)
    back = move(other, lambda i: i ^ 1)
    return mine, back, pairs[:, share + 8 :].reshape(size, extra_rows, width)


def after(value, *earlier):
    return lax.optimization_barrier((value, *earlier))[0] if earlier else value


def expert_kernel(planes, top, place, *refs):
    sources, refs = refs[: 4 * planes], refs[4 * planes :]
    ids, moe_gain, router, hbm_weights, refs = refs[0], refs[1], refs[2], refs[3:9], refs[9:]
    hbm_outs, refs = refs[: 4 * planes], refs[4 * planes :]
    pieces, rows, acts, outs, weights, came, loaded, left_out = refs
    count, half = sources[0].shape
    width = 2 * half
    inputs = [
        pltpu.make_async_copy(source, pieces.at[i], came.at[i]) for i, source in enumerate(sources)
    ]
    units = hbm_weights[0].shape[0]
    loads = [
        pltpu.make_async_copy(
            source.at[pl.ds(part * units // 2, units // 2)],
            weights.at[i, pl.ds(part * units // 2, units // 2)],
            loaded.at[2 * i + part],
        )
        for i, source in enumerate(hbm_weights)
        for part in range(2)
    ]
    for copy in inputs:
        copy.start()
    own = pl.multiple_of(place[1] * half, half)
    rest = pl.multiple_of((1 - place[1]) * half, half)
    gain_own, gain_rest = moe_gain[:, pl.ds(own, half)], moe_gain[:, pl.ds(rest, half)]
    contract = (((1,), (1,)), ((), ()))
    for plane in range(planes):
        for line in range(2):
            inputs[4 * plane + 2 * line].wait()
            inputs[4 * plane + 2 * line + 1].wait()
            if plane == 0:
                loads[2 * line].start()
                loads[2 * line + 1].start()
            left = pieces[4 * plane + 2 * line].astype(jnp.float32)
            right = pieces[4 * plane + 2 * line + 1].astype(jnp.float32)
            total = jnp.sum(left * left, axis=1, keepdims=True) + jnp.sum(
                right * right, axis=1, keepdims=True
            )
            scale = lax.rsqrt(total / width + 1e-06)
            where = pl.ds((2 * plane + line) * count, count)
            rows[where, pl.ds(own, half)] = (left * scale * gain_own).astype(jnp.bfloat16)
            rows[where, pl.ds(rest, half)] = (right * scale * gain_rest).astype(jnp.bfloat16)

    def load(index):
        for part in range(2 * index, 2 * index + 2):
            loads[part].wait()
            if part + 4 < len(loads):
                loads[part + 4].start()

    logits = lax.dot_general(
        router[...], rows[...], (((0,), (1,)), ((), ())), preferred_element_type=jnp.float32
    )
    score = jax.nn.sigmoid(logits)
    experts = score.shape[0]
    number = lax.broadcasted_iota(jnp.int32, (experts, count), 0).astype(jnp.float32)
    shares = []
    for block in range(2 * planes):
        chosen = number == ids[block, 0:1, :]
        for choice in range(1, top):
            chosen = chosen | (number == ids[block, choice : choice + 1, :])
        picked = jnp.where(chosen, score[:, block * count : (block + 1) * count], 0.0)
        shares.append(picked / jnp.sum(picked, axis=0, keepdims=True))
    line = lax.broadcasted_iota(jnp.int32, (count, count), 0)
    lane = lax.broadcasted_iota(jnp.int32, (count, count), 1)
    expert = lax.broadcasted_iota(jnp.int32, (experts, count), 0)
    for which in range(2):
        columns = []
        for share in shares:
            row = jnp.sum(
                jnp.where(expert == place[2 * which], share, 0.0), axis=0, keepdims=True
            )
            columns.append(jnp.sum(jnp.where(line == lane, row, 0.0), axis=1, keepdims=True))
        gate = jnp.concatenate(columns, axis=0)
        load(3 * which)
        gate_proj = lax.dot_general(
            rows[...], weights[3 * which], contract, preferred_element_type=jnp.float32
        )
        load(3 * which + 1)
        up_proj = lax.dot_general(
            rows[...], weights[3 * which + 1], contract, preferred_element_type=jnp.float32
        )
        load(3 * which + 2)
        active = gate_proj / (1.0 + jnp.exp(-gate_proj)) * up_proj
        acts[which] = (active * gate).astype(jnp.bfloat16)
    sends = []
    for side, start in ((1, rest), (0, own)):
        part = jnp.dot(acts[0], weights[2, :, pl.ds(start, half)], preferred_element_type=jnp.float32)
        part += jnp.dot(
            acts[1], weights[5, :, pl.ds(start, half)], preferred_element_type=jnp.float32
        )
        part = part.astype(jnp.bfloat16)
        for plane in range(planes):
            for line in (1, 0):
                index = 4 * plane + 2 * line + side
                first = (2 * plane + line) * count
                outs[index] = part[first : first + count]
                send = pltpu.make_async_copy(outs.at[index], hbm_outs[index], left_out.at[index])
                send.start()
                sends.append(send)
    for send in sends:
        send.wait()


def run_expert(place, pieces, ids, top, moe_gain, router, weights):
    count, half = pieces[0].shape
    planes = len(pieces) // 4
    units, width = weights[0].shape
    rows = 2 * planes * count
    hbm = pl.BlockSpec(memory_space=pltpu.HBM)
    vmem = pl.BlockSpec(memory_space=pltpu.VMEM)
    return pl.pallas_call(
        functools.partial(expert_kernel, planes, top),
        out_shape=[jax.ShapeDtypeStruct((count, half), jnp.bfloat16)] * (4 * planes),
        in_specs=[pl.BlockSpec(memory_space=pltpu.SMEM)]
        + [hbm] * (4 * planes)
        + [vmem] * 3
        + [hbm] * 6,
        out_specs=[hbm] * (4 * planes),
        scratch_shapes=[
            pltpu.VMEM((4 * planes, count, half), jnp.bfloat16),
            pltpu.VMEM((rows, width), jnp.bfloat16),
            pltpu.VMEM((2, rows, units), jnp.bfloat16),
            pltpu.VMEM((4 * planes, count, half), jnp.bfloat16),
            pltpu.VMEM((6, units, width), jnp.bfloat16),
            pltpu.SemaphoreType.DMA((4 * planes,)),
            pltpu.SemaphoreType.DMA((12,)),
            pltpu.SemaphoreType.DMA((4 * planes,)),
        ],
        compiler_params=pltpu.CompilerParams(vmem_limit_bytes=42 * 2**20),
        cost_estimate=pl.CostEstimate(
            flops=2 * 6 * rows * width * units,
            bytes_accessed=2 * (6 * units * width + 8 * planes * count * half),
            transcendentals=2 * rows * units,
        ),
    )(place, *pieces, ids, moe_gain, router, *weights)


def dense_experts(hidden, every_ids, top, moe_gain, router, weights):
    size = lax.axis_size("ctx")
    planes = size // PLANE
    here, side = lax.axis_index("ctx"), lax.axis_index("exp")
    even = here % 2 == 0

    def flip(value, bit):
        return move(value, lambda i: i ^ bit)

    def across(value):
        return lax.ppermute(value, "exp", [(0, 1), (1, 0)])

    def diagonal(value):
        pairs = [
            (i * 2 + x, i * 2 + 1 - x if i % 2 == 0 else (i ^ 2) * 2 + x)
            for i in range(size)
            for x in range(2)
        ]
        return lax.ppermute(value, ("ctx", "exp"), pairs)

    def shift(value, planes_on):
        return move(value, lambda i: (i + PLANE * planes_on) % size)

    weights = [*weights, *(flip(weight, 1) for weight in weights)]
    groups = [[0,1],[2,3]]
    place = jnp.stack([here, side, here ^ 1]).astype(jnp.int32)
    gain = moe_gain[None]
    ties = [(('x', 0), ('z', 3)), (('y', 0), ('z', 3)), (('K', 0), ('turn', 3)), (('z', 2), ('turn', 0)), (('z', 1), ('turn', 0)), (('tox', 0), ('K', 1)), (('tox', 1), ('K', 1))]
    memo = {}

    def get(name, index):
        key = (name, index)
        if key not in memo:
            memo[key] = make(name, index)
        return memo[key]

    def tied(value, name, index):
        return after(value, *[get(*source) for source, target in ties if target == (name, index)])

    def make(name, p):
        if name == "z":
            return hidden if p == 0 else shift(tied(hidden, name, p), -p)
        if name == "x":
            return across(tied(get("z", p), name, p))
        if name == "y":
            return flip(tied(get("z", p), name, p), 2)
        if name == "turn":
            return tied(jnp.where(even, get("y", p), get("x", p)), name, p)
        if name == "diag":
            return diagonal(get("turn", p))
        if name == "outs":
            group = groups[p]
            order = jnp.stack(
                [
                    (here // PLANE + plane) % planes * PLANE + ((here % PLANE) ^ flips)
                    for plane in group
                    for flips in (0, 2)
                ]
            )
            pieces = [get(part, plane) for plane in group for part in ("z", "x", "y", "diag")]
            return run_expert(
                place, pieces, every_ids[order], top, tied(gain, "K", p), router, weights
            )
        if name == "K":
            return get("outs", p)[3]
        group = [g for g in range(len(groups)) if p in groups[g]][0]
        kept, to_x, to_y, corner = get("outs", group)[4 * groups[group].index(p) :][:4]
        if name == "rdiag":
            return diagonal(tied(corner, name, p))
        zero = jnp.zeros_like(corner)
        if name == "toy":
            return to_y + jnp.where(even, get("rdiag", p), zero)
        if name == "tox":
            return to_x + jnp.where(even, zero, get("rdiag", p))
        if name == "sum":
            value = (
                kept.astype(jnp.float32)
                + across(get("tox", p)).astype(jnp.float32)
                + flip(get("toy", p), 2).astype(jnp.float32)
            )
            return value if p == 0 else value.astype(jnp.bfloat16)
        if name == "back":
            value = get("sum", p)
            return value if p == 0 else shift(value, p).astype(jnp.float32)

    total = hidden.astype(jnp.float32)
    for plane in range(planes):
        total = total + get("back", plane)
    return total.astype(jnp.bfloat16)


def run_rows(pieces, w_gate, w_up, w_down):
    row_count = pieces.shape[0] * pieces.shape[1]
    flattened = pieces.reshape(row_count, pieces.shape[2])
    contract = (((1,), (1,)), ((), ()))
    gate_proj = lax.dot_general(flattened, w_gate[0], contract, preferred_element_type=jnp.float32)
    up_proj = lax.dot_general(flattened, w_up[0], contract, preferred_element_type=jnp.float32)
    active = (jax.nn.silu(gate_proj) * up_proj).astype(jnp.bfloat16)
    partial_value = jnp.dot(active, w_down[0], preferred_element_type=jnp.float32).astype(
        jnp.bfloat16
    )
    full_width = partial_value.shape[1]
    shaped = partial_value.reshape(pieces.shape[0], pieces.shape[1], full_width)
    return lax.all_to_all(shaped, "ctx", split_axis=0, concat_axis=0, tiled=True)


def columns_of(rows):
    pad = jnp.zeros((-rows.shape[0] % 128, rows.shape[1]), rows.dtype)
    return jnp.concatenate([rows, pad], axis=0).T if pad.shape[0] else rows.T


def state_kernel(step, rate, x, b, state, running):
    heads, count = step.shape
    groups = b.shape[1] // N
    per_group = heads // groups
    wide = per_group * P_SIZE
    total = -step[...] * rate[...]
    lane = lax.broadcasted_iota(jnp.int32, (heads, count), 1)
    hop = 1
    while hop < count:
        total = total + jnp.where(lane >= hop, pltpu.roll(total, hop, 1), 0.0)
        hop *= 2
    running[...] = total
    weight = jnp.exp(total[:, count - 1 :] - total) * step[...]
    for group in range(groups):
        turned = x[:, group * wide : (group + 1) * wide].astype(jnp.float32).T
        carried = jnp.concatenate(
            [
                turned[q * P_SIZE : (q + 1) * P_SIZE]
                * weight[group * per_group + q : group * per_group + q + 1]
                for q in range(per_group)
            ],
            axis=0,
        ).astype(jnp.bfloat16)
        state[group * wide : (group + 1) * wide] = jnp.dot(
            carried, b[:, group * N : (group + 1) * N], preferred_element_type=jnp.float32
        )


def inner_kernel(step, running, x, b, c, inner):
    heads, count = step.shape
    groups = b.shape[1] // N
    per_group = heads // groups
    total = running[...]
    columns = columns_of(total)
    line = lax.broadcasted_iota(jnp.int32, (count, count), 0)
    lane = lax.broadcasted_iota(jnp.int32, (count, count), 1)
    first = lax.broadcasted_iota(jnp.int32, (count, 2 * P_SIZE), 1) < P_SIZE
    for group in range(groups):
        where = slice(group * N, (group + 1) * N)
        scores = lax.dot_general(
            c[:, where], b[:, where], (((1,), (1,)), ((), ())), preferred_element_type=jnp.float32
        )
        scores = jnp.where(line >= lane, scores, 0.0)
        for pair in range(per_group // 2):
            head = group * per_group + 2 * pair
            mixing = []
            for h in (head, head + 1):
                spread = columns[:, h : h + 1] - total[h : h + 1]
                decay = jnp.exp(jnp.where(line >= lane, spread, 0.0))
                mixing.append((decay * scores * step[h : h + 1]).astype(jnp.bfloat16))
            both = x[:, head * P_SIZE : (head + 2) * P_SIZE].astype(jnp.float32)
            apart = jnp.concatenate(
                [jnp.where(first, both, 0.0), jnp.where(first, 0.0, both)], axis=0
            )
            inner[:, head * P_SIZE : (head + 2) * P_SIZE] = jnp.dot(
                jnp.concatenate(mixing, axis=1),
                apart.astype(jnp.bfloat16),
                preferred_element_type=jnp.float32,
            )


def mixer_kernel(
    place, mine, back, c, inner, running, z, gain, weight, stream, own, theirs, high, low, normed
):
    heads, count = running.shape
    groups = c.shape[1] // N
    per_group = heads // groups
    wide = per_group * P_SIZE
    half = mine.shape[0]
    odd = place[0] % 2
    for part in range(2):
        value = jnp.where(odd == part, mine[...], back[...])
        rounded = value.astype(jnp.bfloat16)
        high[part * half : (part + 1) * half] = rounded
        low[part * half : (part + 1) * half] = (value - rounded.astype(jnp.float32)).astype(
            jnp.bfloat16
        )
    growth = columns_of(jnp.exp(running[...]))
    first = lax.broadcasted_iota(jnp.int32, (count, 2 * P_SIZE), 1) < P_SIZE
    contract = (((1,), (1,)), ((), ()))
    for group in range(groups):
        where = slice(group * wide, (group + 1) * wide)
        reads = c[:, group * N : (group + 1) * N]
        carried = lax.dot_general(
            reads, high[where], contract, preferred_element_type=jnp.float32
        ) + lax.dot_general(reads, low[where], contract, preferred_element_type=jnp.float32)
        heads_in = range(group * per_group, (group + 1) * per_group, 2)
        scale = jnp.concatenate(
            [jnp.where(first, growth[:, h : h + 1], growth[:, h + 1 : h + 2]) for h in heads_in],
            axis=1,
        )
        gate = z[:, where].astype(jnp.float32)
        gated = (inner[:, where] + scale * carried) * (gate / (1.0 + jnp.exp(-gate)))
        mean = jnp.sum(gated * gated, axis=1, keepdims=True) / wide
        normed[:, where] = (gated * lax.rsqrt(mean + 1e-05) * gain[:, where]).astype(jnp.bfloat16)
    width = stream.shape[1]
    shares = theirs.shape[0] + 1
    for step in range(shares - 1, -1, -1):
        start = pl.multiple_of(lax.rem(place[1] + step, shares) * width, width)
        part = jnp.dot(
            normed[...], weight[:, pl.ds(start, width)], preferred_element_type=jnp.float32
        )
        if step:
            theirs[step - 1] = part.astype(jnp.bfloat16)
        else:
            own[...] = part + stream[...].astype(jnp.float32)


def per_device(
    ssm_input,
    gate_input,
    b_input,
    c_input,
    step_size,
    decay_rate,
    norm_gain,
    out_weight,
    stream,
    moe_gain,
    router,
    expert_ids,
    w_gate,
    w_up,
    w_down,
):
    token_count, inner_width = ssm_input.shape
    head_count = step_size.shape[0]
    slice_width = stream.shape[1]
    expert_count = router.shape[1]
    top_count = expert_ids.shape[1]
    exp_size = lax.axis_size("exp")
    capacity = max(
        2, token_count * top_count // expert_count + token_count * top_count // (4 * expert_count)
    )
    vmem = pl.BlockSpec(memory_space=pltpu.VMEM)
    wide = jax.ShapeDtypeStruct((token_count, inner_width), jnp.float32)
    state, running = pl.pallas_call(
        state_kernel,
        out_shape=[
            jax.ShapeDtypeStruct((inner_width, N), jnp.float32),
            jax.ShapeDtypeStruct(step_size.shape, jnp.float32),
        ],
        in_specs=[vmem] * 4,
        out_specs=[vmem] * 2,
        compiler_params=pltpu.CompilerParams(vmem_limit_bytes=16 * 2**20),
    )(step_size, decay_rate[:, None], ssm_input, b_input)
    id_rows = jnp.pad(expert_ids.T.astype(jnp.float32), ((0, -expert_ids.shape[1] % 8), (0, 0)))
    mine, back, every_ids = prefix_states(state, running[:, -1], id_rows)
    inner = pl.pallas_call(
        inner_kernel,
        out_shape=wide,
        in_specs=[vmem] * 5,
        out_specs=vmem,
        compiler_params=pltpu.CompilerParams(vmem_limit_bytes=16 * 2**20),
    )(step_size, running, ssm_input, b_input, c_input)
    place = jnp.stack([lax.axis_index("ctx"), lax.axis_index("exp")]).astype(jnp.int32)
    hidden_own, theirs = pl.pallas_call(
        mixer_kernel,
        out_shape=[
            jax.ShapeDtypeStruct(stream.shape, jnp.float32),
            jax.ShapeDtypeStruct((exp_size - 1, *stream.shape), jnp.bfloat16),
        ],
        in_specs=[pl.BlockSpec(memory_space=pltpu.SMEM)] + [vmem] * 9,
        out_specs=[vmem] * 2,
        scratch_shapes=[
            pltpu.VMEM((inner_width, N), jnp.bfloat16),
            pltpu.VMEM((inner_width, N), jnp.bfloat16),
            pltpu.VMEM((token_count, inner_width), jnp.bfloat16),
        ],
        compiler_params=pltpu.CompilerParams(vmem_limit_bytes=24 * 2**20),
    )(place, mine, back, c_input, inner, running, gate_input, norm_gain[None], out_weight, stream)
    for step in range(1, exp_size):
        ring = [(i, (i + step) % exp_size) for i in range(exp_size)]
        sent = lax.ppermute(theirs[step - 1], "exp", ring)
        hidden_own = hidden_own + sent.astype(jnp.float32)
    hidden_own = hidden_own.astype(jnp.bfloat16)
    every_token = token_count * lax.axis_size("ctx")
    if exp_size == 2 and every_token <= 3 * expert_count * capacity:
        return dense_experts(
            hidden_own,
            every_ids,
            top_count,
            moe_gain,
            router,
            (w_gate[0], w_up[0], w_down[0]),
        )
    hidden_all = lax.all_gather(hidden_own, "exp", axis=1, tiled=True)
    hidden_f = hidden_all.astype(jnp.float32)
    mean_h = jnp.mean(hidden_f * hidden_f, axis=1, keepdims=True)
    sent_rows = (hidden_f * lax.rsqrt(mean_h + 1e-06) * moe_gain).astype(jnp.bfloat16)
    logits = jnp.dot(sent_rows, router, preferred_element_type=jnp.float32)
    sigmoid_score = jax.nn.sigmoid(logits)
    expert_range = jnp.arange(expert_count, dtype=jnp.int32)
    matches = expert_ids[:, :, None] == expert_range
    picked = jnp.sum(jnp.where(matches, sigmoid_score[:, None, :], 0.0), axis=2)
    gates = picked / jnp.sum(picked, axis=1, keepdims=True)
    flat_ids = expert_ids.reshape(-1)
    one_hot = (flat_ids[:, None] == expert_range).astype(jnp.int32)
    slot_index = jnp.sum((jnp.cumsum(one_hot, axis=0) - one_hot) * one_hot, axis=1)
    target = flat_ids * capacity + slot_index
    token_of = jnp.arange(token_count * top_count, dtype=jnp.int32) // top_count
    source_row = (
        jnp.full((expert_count * capacity,), token_count, jnp.int32).at[target].set(token_of)
    )
    padded = jnp.concatenate([sent_rows, jnp.zeros((1, sent_rows.shape[1]), jnp.bfloat16)], axis=0)
    outgoing = padded[source_row].reshape(expert_count, capacity, sent_rows.shape[1])
    returned = run_rows(
        lax.all_to_all(outgoing, "ctx", split_axis=0, concat_axis=0, tiled=True),
        w_gate,
        w_up,
        w_down,
    )
    back_width = returned.shape[2]
    flat_back = returned.reshape(expert_count * capacity, back_width)
    slot_rows = target.reshape(token_count, top_count)
    moe_part = jnp.zeros((token_count, back_width), jnp.float32)
    for choice_number in range(top_count):
        picked_rows = flat_back[slot_rows[:, choice_number]].astype(jnp.float32)
        moe_part = moe_part + gates[:, choice_number][:, None] * picked_rows
    moe_sum = lax.psum_scatter(
        moe_part.astype(jnp.bfloat16), "exp", scatter_dimension=1, tiled=True
    ).astype(jnp.float32)
    return (hidden_own.astype(jnp.float32) + moe_sum).astype(jnp.bfloat16)


def solution(mesh):
    in_specs = (
        P("ctx", "exp"),
        P("ctx", "exp"),
        P("ctx", "exp"),
        P("ctx", "exp"),
        P("exp", "ctx"),
        P("exp"),
        P("exp"),
        P("exp", None),
        P("ctx", "exp"),
        P(),
        P(),
        P("ctx", None),
        P("ctx", "exp", None),
        P("ctx", "exp", None),
        P("ctx", "exp", None),
    )
    out_specs = P("ctx", "exp")
    return jax.shard_map(
        per_device, mesh=mesh, in_specs=in_specs, out_specs=out_specs, check_vma=False
    )
```

```python
import functools

import jax
import jax.numpy as jnp
from jax import lax
from jax.experimental import pallas as pl
from jax.experimental.pallas import tpu as pltpu
from jax.sharding import PartitionSpec as P

P_SIZE = 64
N = 128
PLANE = 4


def move(value, partner):
    return lax.ppermute(value, "ctx", [(i, partner(i)) for i in range(lax.axis_size("ctx"))])


def as_rows(flat, width):
    tile = 8 * width
    return jnp.pad(flat, (0, -flat.shape[0] % tile)).reshape(-1, width)


def chain_kernel(pairs, out):
    count, share, width = out.shape
    line = lax.broadcasted_iota(jnp.int32, (share, width), 0)
    lane = lax.broadcasted_iota(jnp.int32, (share, width), 1)
    entering = jnp.zeros((share, width), jnp.float32)
    for pair in range(count):
        out[pair] = entering
        logs = jnp.where(line == lane, pairs[pair, share : share + 1, :], 0.0)
        decay = jnp.exp(jnp.sum(logs, axis=1, keepdims=True))
        entering = decay * entering + pairs[pair, :share]


def prefix_states(state, log_total, extra):
    size = lax.axis_size("ctx")
    odd = lax.axis_index("ctx") % 2 == 1
    rows, width = state.shape
    half = rows // 2
    share = rows // size
    extra_rows = extra.shape[0]
    row_log = jnp.repeat(log_total, rows // log_total.shape[0])

    def halves(array):
        return array[:half], array[half:]

    def pick(flag, first, second):
        return jnp.where(flag, second, first)

    low, high = halves(state)
    log_low, log_high = halves(row_log)
    kept, given = pick(odd, low, high), pick(odd, high, low)
    kept_log, given_log = pick(odd, log_low, log_high), pick(odd, log_high, log_low)
    log_rows = as_rows(given_log, width)
    got = move(jnp.concatenate([given, log_rows, extra], axis=0), lambda i: i ^ 1)
    got_log = got[half : half + log_rows.shape[0]].reshape(-1)[:half]
    got_extra = got[half + log_rows.shape[0] :]
    got = got[:half]
    first, second = pick(odd, kept, got), pick(odd, got, kept)
    first_log, second_log = pick(odd, kept_log, got_log), pick(odd, got_log, kept_log)
    pair_extra = jnp.concatenate([pick(odd, extra, got_extra), pick(odd, got_extra, extra)], axis=0)
    pair_state = jnp.exp(second_log)[:, None] * first + second
    pair_log = (first_log + second_log).reshape(size // 2, 1, share)
    pair_log = jnp.pad(pair_log, ((0, 0), (0, 7), (0, width - share)))
    pair_extra = jnp.broadcast_to(pair_extra[None], (size // 2, 2 * extra_rows, width))
    sent = jnp.concatenate(
        [pair_state.reshape(size // 2, share, width), pair_log, pair_extra], axis=1
    )
    groups = [[i for i in range(size) if i % 2 == k] for k in range(2)]

    def exchange(array):
        return lax.all_to_all(
            array, "ctx", split_axis=0, concat_axis=0, axis_index_groups=groups, tiled=True
        )

    pairs = exchange(sent)
    found = pl.pallas_call(
        chain_kernel, out_shape=jax.ShapeDtypeStruct((size // 2, share, width), jnp.float32)
    )(pairs)
    into_first = exchange(found).reshape(half, width)
    into_second = jnp.exp(first_log)[:, None] * into_first + first
    mine, other = pick(odd, into_first, into_second), pick(odd, into_second, into_first)
    back = move(other, lambda i: i ^ 1)
    return mine, back, pairs[:, share + 8 :].reshape(size, extra_rows, width)


def expert_kernel(planes, top, place, *refs):
    sources, refs = refs[: 4 * planes], refs[4 * planes :]
    ids, moe_gain, router, hbm_weights, refs = refs[0], refs[1], refs[2], refs[3:9], refs[9:]
    hbm_outs, refs = refs[: 4 * planes], refs[4 * planes :]
    rows, acts, weights, loaded = refs
    pieces, outs = sources, hbm_outs
    units = weights.shape[1]
    loads = [
        pltpu.make_async_copy(
            hbm_weights[i].at[pl.ds(part * units // 2, units // 2)],
            weights.at[i, pl.ds(part * units // 2, units // 2)],
            loaded.at[2 * i + part],
        )
        for i in (0, 1, 3, 4, 2, 5)
        for part in range(2)
    ]
    for copy in loads[:6]:
        copy.start()

    def load(index):
        for part in range(2 * index, 2 * index + 2):
            loads[part].wait()
            if part + 6 < len(loads):
                loads[part + 6].start()

    count, half = sources[0].shape
    width = 2 * half
    own = pl.multiple_of(place[1] * half, half)
    rest = pl.multiple_of((1 - place[1]) * half, half)
    gain_own, gain_rest = moe_gain[:, pl.ds(own, half)], moe_gain[:, pl.ds(rest, half)]
    contract = (((1,), (1,)), ((), ()))
    for plane in range(planes):
        for line in range(2):
            left = pieces[4 * plane + 2 * line][...].astype(jnp.float32)
            right = pieces[4 * plane + 2 * line + 1][...].astype(jnp.float32)
            total = jnp.sum(left * left, axis=1, keepdims=True) + jnp.sum(
                right * right, axis=1, keepdims=True
            )
            scale = lax.rsqrt(total / width + 1e-06)
            where = pl.ds((2 * plane + line) * count, count)
            rows[where, pl.ds(own, half)] = (left * scale * gain_own).astype(jnp.bfloat16)
            rows[where, pl.ds(rest, half)] = (right * scale * gain_rest).astype(jnp.bfloat16)

    logits = lax.dot_general(
        router[...], rows[...], (((0,), (1,)), ((), ())), preferred_element_type=jnp.float32
    )
    score = jax.nn.sigmoid(logits)
    experts = score.shape[0]
    number = lax.broadcasted_iota(jnp.int32, (experts, count), 0).astype(jnp.float32)
    shares = []
    for block in range(2 * planes):
        chosen = number == ids[block, 0:1, :]
        for choice in range(1, top):
            chosen = chosen | (number == ids[block, choice : choice + 1, :])
        picked = jnp.where(chosen, score[:, block * count : (block + 1) * count], 0.0)
        shares.append(picked / jnp.sum(picked, axis=0, keepdims=True))
    line = lax.broadcasted_iota(jnp.int32, (count, count), 0)
    lane = lax.broadcasted_iota(jnp.int32, (count, count), 1)
    expert = lax.broadcasted_iota(jnp.int32, (experts, count), 0)
    for which in range(2):
        columns = []
        for share in shares:
            row = jnp.sum(
                jnp.where(expert == place[2 * which], share, 0.0), axis=0, keepdims=True
            )
            columns.append(jnp.sum(jnp.where(line == lane, row, 0.0), axis=1, keepdims=True))
        gate = jnp.concatenate(columns, axis=0)
        load(2 * which)
        gate_proj = lax.dot_general(
            rows[...], weights[3 * which], contract, preferred_element_type=jnp.float32
        )
        load(2 * which + 1)
        up_proj = lax.dot_general(
            rows[...], weights[3 * which + 1], contract, preferred_element_type=jnp.float32
        )
        active = gate_proj / (1.0 + jnp.exp(-gate_proj)) * up_proj
        acts[which] = (active * gate).astype(jnp.bfloat16)
    load(4)
    load(5)
    for side, start in ((1, rest), (0, own)):
        part = jnp.dot(acts[0], weights[2, :, pl.ds(start, half)], preferred_element_type=jnp.float32)
        part += jnp.dot(
            acts[1], weights[5, :, pl.ds(start, half)], preferred_element_type=jnp.float32
        )
        part = part.astype(jnp.bfloat16)
        for plane in range(planes):
            for line in (1, 0):
                index = 4 * plane + 2 * line + side
                first = (2 * plane + line) * count
                outs[index][...] = part[first : first + count]


def run_expert(place, pieces, ids, top, moe_gain, router, weights):
    count, half = pieces[0].shape
    planes = len(pieces) // 4
    units, width = weights[0].shape
    rows = 2 * planes * count
    vmem = pl.BlockSpec(memory_space=pltpu.VMEM)
    return pl.pallas_call(
        functools.partial(expert_kernel, planes, top),
        out_shape=[jax.ShapeDtypeStruct((count, half), jnp.bfloat16)] * (4 * planes),
        in_specs=[pl.BlockSpec(memory_space=pltpu.SMEM)]
        + [vmem] * (4 * planes)
        + [vmem] * 3
        + [pl.BlockSpec(memory_space=pltpu.HBM)] * 6,
        out_specs=[vmem] * (4 * planes),
        scratch_shapes=[
            pltpu.VMEM((rows, width), jnp.bfloat16),
            pltpu.VMEM((2, rows, units), jnp.bfloat16),
            pltpu.VMEM((6, units, width), jnp.bfloat16),
            pltpu.SemaphoreType.DMA((12,)),
        ],
        compiler_params=pltpu.CompilerParams(vmem_limit_bytes=56 * 2**20),
        cost_estimate=pl.CostEstimate(
            flops=2 * 6 * rows * width * units,
            bytes_accessed=2 * (6 * units * width + 8 * planes * count * half),
            transcendentals=2 * rows * units,
        ),
    )(place, *pieces, ids, moe_gain, router, *weights)


def dense_experts(hidden, every_ids, top, moe_gain, router, weights):
    size = lax.axis_size("ctx")
    planes = size // PLANE
    here, side = lax.axis_index("ctx"), lax.axis_index("exp")
    even = here % 2 == 0

    def flip(value, bit):
        return move(value, lambda i: i ^ bit)

    def across(value):
        return lax.ppermute(value, "exp", [(0, 1), (1, 0)])

    def diagonal(value):
        pairs = [
            (i * 2 + x, i * 2 + 1 - x if i % 2 == 0 else (i ^ 2) * 2 + x)
            for i in range(size)
            for x in range(2)
        ]
        return lax.ppermute(value, ("ctx", "exp"), pairs)

    def shift(value, planes_on):
        return move(value, lambda i: (i + PLANE * planes_on) % size)

    weights = [*weights, *(flip(weight, 1) for weight in weights)]
    groups = [[0],[1],[2],[3]]
    phases = [
        [("x", 0), ("y", 0)],
        [("diag", 0), ("z", 1)],
        [("K", 0), ("x", 1), ("y", 1), ("z", 2)],
        [("diag", 1), ("x", 2), ("y", 2), ("z", 3)],
        [("K", 1), ("x", 3), ("y", 3), ("diag", 2), ("rdiag", 0)],
        [("K", 2), ("diag", 3), ("rx", 0), ("ry", 0), ("rdiag", 1)],
        [("K", 3), ("rx", 1), ("ry", 1), ("rdiag", 2)],
        [("rx", 2), ("ry", 2), ("rdiag", 3), ("rz", 1)],
        [("rx", 3), ("ry", 3), ("rz", 2)],
        [("rz", 3)],
    ]
    place = jnp.stack([here, side, here ^ 1]).astype(jnp.int32)
    done = {("z", 0): hidden}

    def operands(name, p):
        if name == "z":
            return [done["z", 0]]
        if name in ("x", "y"):
            return [done["z", p]]
        if name == "diag":
            return [jnp.where(even, done["y", p], done["x", p])]
        if name == "K":
            return [done[part, q] for q in groups[p] for part in ("z", "x", "y", "diag")]
        group = [g for g in range(len(groups)) if p in groups[g]][0]
        kept, to_x, to_y, corner = done["K", group][4 * groups[group].index(p) :][:4]
        if name == "rdiag":
            return [corner]
        zero = jnp.zeros_like(corner)
        if name == "rx":
            return [to_x + jnp.where(even, zero, done["rdiag", p])]
        if name == "ry":
            return [to_y + jnp.where(even, done["rdiag", p], zero)]
        parts = (kept, done["rx", p], done["ry", p])
        return [sum(part.astype(jnp.float32) for part in parts).astype(jnp.bfloat16)]

    def run(name, p, values):
        if name in ("z", "rz"):
            return [shift(values[0], -p if name == "z" else p)]
        if name in ("x", "rx"):
            return [across(values[0])]
        if name in ("y", "ry"):
            return [flip(values[0], 2)]
        if name in ("diag", "rdiag"):
            return [diagonal(values[0])]
        order = jnp.stack(
            [
                (here // PLANE + plane) % planes * PLANE + ((here % PLANE) ^ flips)
                for plane in groups[p]
                for flips in (0, 2)
            ]
        )
        return run_expert(place, values, every_ids[order], top, moe_gain[None], router, weights)

    for phase in phases:
        outs = [run(*step, operands(*step)) for step in phase]
        flat = [value for values in outs for value in values]
        held = list(lax.optimization_barrier((done["z", 0], *flat)))
        done["z", 0] = held.pop(0)
        for step, values in zip(phase, outs):
            values = [held.pop(0) for _ in values]
            done[step] = values if step[0] == "K" else values[0]
    total = hidden.astype(jnp.float32)
    group = [g for g in range(len(groups)) if 0 in groups[g]][0]
    total = total + done["K", group][4 * groups[group].index(0)].astype(jnp.float32)
    total = total + done["rx", 0].astype(jnp.float32) + done["ry", 0].astype(jnp.float32)
    for plane in range(1, planes):
        total = total + done["rz", plane].astype(jnp.float32)
    return total.astype(jnp.bfloat16)


def run_rows(pieces, w_gate, w_up, w_down):
    row_count = pieces.shape[0] * pieces.shape[1]
    flattened = pieces.reshape(row_count, pieces.shape[2])
    contract = (((1,), (1,)), ((), ()))
    gate_proj = lax.dot_general(flattened, w_gate[0], contract, preferred_element_type=jnp.float32)
    up_proj = lax.dot_general(flattened, w_up[0], contract, preferred_element_type=jnp.float32)
    active = (jax.nn.silu(gate_proj) * up_proj).astype(jnp.bfloat16)
    partial_value = jnp.dot(active, w_down[0], preferred_element_type=jnp.float32).astype(
        jnp.bfloat16
    )
    full_width = partial_value.shape[1]
    shaped = partial_value.reshape(pieces.shape[0], pieces.shape[1], full_width)
    return lax.all_to_all(shaped, "ctx", split_axis=0, concat_axis=0, tiled=True)


def columns_of(rows):
    pad = jnp.zeros((-rows.shape[0] % 128, rows.shape[1]), rows.dtype)
    return jnp.concatenate([rows, pad], axis=0).T if pad.shape[0] else rows.T


def column_of(row):
    size = row.shape[1]
    line = lax.broadcasted_iota(jnp.int32, (size, size), 0)
    lane = lax.broadcasted_iota(jnp.int32, (size, size), 1)
    return jnp.sum(jnp.where(line == lane, row, 0.0), axis=1, keepdims=True)


def state_kernel(rate, step_hbm, x_hbm, b_hbm, state, running, step, x, b, came):
    copies = [
        pltpu.make_async_copy(source, target, came.at[i])
        for i, (source, target) in enumerate(((step_hbm, step), (x_hbm, x), (b_hbm, b)))
    ]
    for copy in copies:
        copy.start()
    heads, count = step.shape
    groups = b.shape[1] // N
    per_group = heads // groups
    wide = per_group * P_SIZE
    copies[0].wait()
    total = -step[...] * column_of(rate[...])
    lane = lax.broadcasted_iota(jnp.int32, (heads, count), 1)
    hop = 1
    while hop < count:
        total = total + jnp.where(lane >= hop, pltpu.roll(total, hop, 1), 0.0)
        hop *= 2
    running[...] = total
    weight = jnp.exp(total[:, count - 1 :] - total) * step[...]
    copies[1].wait()
    copies[2].wait()
    for group in range(groups):
        turned = x[:, group * wide : (group + 1) * wide].astype(jnp.float32).T
        carried = jnp.concatenate(
            [
                turned[q * P_SIZE : (q + 1) * P_SIZE]
                * weight[group * per_group + q : group * per_group + q + 1]
                for q in range(per_group)
            ],
            axis=0,
        ).astype(jnp.bfloat16)
        state[group * wide : (group + 1) * wide] = jnp.dot(
            carried, b[:, group * N : (group + 1) * N], preferred_element_type=jnp.float32
        )


def inner_part(step, running, x, b, c, inner):
    heads, count = step.shape
    groups = b.shape[1] // N
    per_group = heads // groups
    total = running[...]
    columns = columns_of(total)
    line = lax.broadcasted_iota(jnp.int32, (count, count), 0)
    lane = lax.broadcasted_iota(jnp.int32, (count, count), 1)
    first = lax.broadcasted_iota(jnp.int32, (count, 2 * P_SIZE), 1) < P_SIZE
    for group in range(groups):
        where = slice(group * N, (group + 1) * N)
        scores = lax.dot_general(
            c[:, where], b[:, where], (((1,), (1,)), ((), ())), preferred_element_type=jnp.float32
        )
        scores = jnp.where(line >= lane, scores, 0.0)
        for pair in range(per_group // 2):
            head = group * per_group + 2 * pair
            mixing = []
            for h in (head, head + 1):
                spread = columns[:, h : h + 1] - total[h : h + 1]
                decay = jnp.exp(jnp.where(line >= lane, spread, 0.0))
                mixing.append((decay * scores * step[h : h + 1]).astype(jnp.bfloat16))
            both = x[:, head * P_SIZE : (head + 2) * P_SIZE].astype(jnp.float32)
            apart = jnp.concatenate(
                [jnp.where(first, both, 0.0), jnp.where(first, 0.0, both)], axis=0
            )
            inner[:, head * P_SIZE : (head + 2) * P_SIZE] = jnp.dot(
                jnp.concatenate(mixing, axis=1),
                apart.astype(jnp.bfloat16),
                preferred_element_type=jnp.float32,
            )


def project(place, rows, weight_hbm, weight, came, first, last, give):
    shares, _, width = weight.shape
    total = weight_hbm.shape[1] // width
    copies = []
    for step in range(first, last):
        start = pl.multiple_of(lax.rem(place[1] + step, total) * width, width)
        copies.append(
            pltpu.make_async_copy(
                weight_hbm.at[:, pl.ds(start, width)], weight.at[step - first], came.at[step - first]
            )
        )
    yield [copy.start() for copy in copies]
    for step in range(first, last):
        copies[step - first].wait()
        give(
            step,
            jnp.dot(rows[...], weight[step - first], preferred_element_type=jnp.float32),
        )
    yield


def own_kernel(place, normed, weight_hbm, stream, own, weight, came):
    def give(step, part):
        own[...] = part + stream[...].astype(jnp.float32)

    for _ in project(place, normed, weight_hbm, weight, came, 0, 1, give):
        pass


def mixer_kernel(place, gain, weight_hbm, *refs):
    sources, (normed, theirs), refs = refs[:8], refs[8:10], refs[10:]
    targets, (inner, high, low, weight, came, fetched) = refs[:8], refs[8:]
    fetches = [
        pltpu.make_async_copy(source, target, fetched.at[i])
        for i, (source, target) in enumerate(zip(sources, targets))
    ]
    for fetch in fetches:
        fetch.start()
    step, running, x, b, c, z, mine, back = targets

    def give(step, part):
        theirs[step - 1] = part.astype(jnp.bfloat16)

    projection = project(
        place, normed, weight_hbm, weight, came, 1, theirs.shape[0] + 1, give
    )
    next(projection)
    for fetch in fetches[:5]:
        fetch.wait()
    inner_part(step, running, x, b, c, inner)
    for fetch in fetches[5:]:
        fetch.wait()
    heads, count = running.shape
    groups = c.shape[1] // N
    per_group = heads // groups
    wide = per_group * P_SIZE
    half = mine.shape[0]
    odd = place[0] % 2
    for part in range(2):
        value = jnp.where(odd == part, mine[...], back[...])
        rounded = value.astype(jnp.bfloat16)
        high[part * half : (part + 1) * half] = rounded
        low[part * half : (part + 1) * half] = (value - rounded.astype(jnp.float32)).astype(
            jnp.bfloat16
        )
    growth = columns_of(jnp.exp(running[...]))
    first = lax.broadcasted_iota(jnp.int32, (count, 2 * P_SIZE), 1) < P_SIZE
    contract = (((1,), (1,)), ((), ()))
    for group in range(groups):
        where = slice(group * wide, (group + 1) * wide)
        reads = c[:, group * N : (group + 1) * N]
        carried = lax.dot_general(
            reads, high[where], contract, preferred_element_type=jnp.float32
        ) + lax.dot_general(reads, low[where], contract, preferred_element_type=jnp.float32)
        heads_in = range(group * per_group, (group + 1) * per_group, 2)
        scale = jnp.concatenate(
            [jnp.where(first, growth[:, h : h + 1], growth[:, h + 1 : h + 2]) for h in heads_in],
            axis=1,
        )
        gate = z[:, where].astype(jnp.float32)
        gated = (inner[:, where] + scale * carried) * (gate / (1.0 + jnp.exp(-gate)))
        mean = jnp.sum(gated * gated, axis=1, keepdims=True) / wide
        normed[:, where] = (gated * lax.rsqrt(mean + 1e-05) * gain[:, where]).astype(jnp.bfloat16)
    next(projection)


def per_device(
    ssm_input,
    gate_input,
    b_input,
    c_input,
    step_size,
    decay_rate,
    norm_gain,
    out_weight,
    stream,
    moe_gain,
    router,
    expert_ids,
    w_gate,
    w_up,
    w_down,
):
    token_count, inner_width = ssm_input.shape
    head_count = step_size.shape[0]
    slice_width = stream.shape[1]
    expert_count = router.shape[1]
    top_count = expert_ids.shape[1]
    exp_size = lax.axis_size("exp")
    capacity = max(
        2, token_count * top_count // expert_count + token_count * top_count // (4 * expert_count)
    )
    vmem = pl.BlockSpec(memory_space=pltpu.VMEM)
    hbm = pl.BlockSpec(memory_space=pltpu.HBM)
    state, running = pl.pallas_call(
        state_kernel,
        out_shape=[
            jax.ShapeDtypeStruct((inner_width, N), jnp.float32),
            jax.ShapeDtypeStruct(step_size.shape, jnp.float32),
        ],
        in_specs=[vmem] + [hbm] * 3,
        out_specs=[vmem] * 2,
        scratch_shapes=[
            pltpu.VMEM(step_size.shape, jnp.float32),
            pltpu.VMEM(ssm_input.shape, jnp.bfloat16),
            pltpu.VMEM(b_input.shape, jnp.bfloat16),
            pltpu.SemaphoreType.DMA((3,)),
        ],
        compiler_params=pltpu.CompilerParams(vmem_limit_bytes=16 * 2**20),
    )(decay_rate[None], step_size, ssm_input, b_input)
    id_rows = jnp.pad(expert_ids.T.astype(jnp.float32), ((0, -expert_ids.shape[1] % 8), (0, 0)))
    mine, back, every_ids = prefix_states(state, running[:, -1], id_rows)
    place = jnp.stack([lax.axis_index("ctx"), lax.axis_index("exp")]).astype(jnp.int32)
    fetched = (step_size, running, ssm_input, b_input, c_input, gate_input, mine, back)
    normed, theirs = pl.pallas_call(
        mixer_kernel,
        out_shape=[
            jax.ShapeDtypeStruct((token_count, inner_width), jnp.bfloat16),
            jax.ShapeDtypeStruct((exp_size - 1, *stream.shape), jnp.bfloat16),
        ],
        in_specs=[pl.BlockSpec(memory_space=pltpu.SMEM), vmem] + [hbm] * 9,
        out_specs=[vmem] * 2,
        scratch_shapes=[pltpu.VMEM(array.shape, array.dtype) for array in fetched]
        + [
            pltpu.VMEM((token_count, inner_width), jnp.float32),
            pltpu.VMEM((inner_width, N), jnp.bfloat16),
            pltpu.VMEM((inner_width, N), jnp.bfloat16),
            pltpu.VMEM((exp_size - 1, inner_width, slice_width), jnp.bfloat16),
            pltpu.SemaphoreType.DMA((exp_size - 1,)),
            pltpu.SemaphoreType.DMA((8,)),
        ],
        compiler_params=pltpu.CompilerParams(vmem_limit_bytes=60 * 2**20),
    )(place, norm_gain[None], out_weight, *fetched)
    hidden_own = pl.pallas_call(
        own_kernel,
        out_shape=jax.ShapeDtypeStruct(stream.shape, jnp.float32),
        in_specs=[pl.BlockSpec(memory_space=pltpu.SMEM), vmem, hbm, vmem],
        out_specs=vmem,
        scratch_shapes=[
            pltpu.VMEM((1, inner_width, slice_width), jnp.bfloat16),
            pltpu.SemaphoreType.DMA((1,)),
        ],
        compiler_params=pltpu.CompilerParams(vmem_limit_bytes=60 * 2**20),
        cost_estimate=pl.CostEstimate(
            flops=2 * token_count * inner_width * slice_width,
            bytes_accessed=2 * inner_width * slice_width,
            transcendentals=0,
        ),
    )(place, normed, out_weight, stream)
    for step in range(1, exp_size):
        ring = [(i, (i + step) % exp_size) for i in range(exp_size)]
        sent = lax.ppermute(theirs[step - 1], "exp", ring)
        hidden_own = hidden_own + sent.astype(jnp.float32)
    hidden_own = hidden_own.astype(jnp.bfloat16)
    every_token = token_count * lax.axis_size("ctx")
    if exp_size == 2 and every_token <= 3 * expert_count * capacity:
        return dense_experts(
            hidden_own,
            every_ids,
            top_count,
            moe_gain,
            router,
            (w_gate[0], w_up[0], w_down[0]),
        )
    hidden_all = lax.all_gather(hidden_own, "exp", axis=1, tiled=True)
    hidden_f = hidden_all.astype(jnp.float32)
    mean_h = jnp.mean(hidden_f * hidden_f, axis=1, keepdims=True)
    sent_rows = (hidden_f * lax.rsqrt(mean_h + 1e-06) * moe_gain).astype(jnp.bfloat16)
    logits = jnp.dot(sent_rows, router, preferred_element_type=jnp.float32)
    sigmoid_score = jax.nn.sigmoid(logits)
    expert_range = jnp.arange(expert_count, dtype=jnp.int32)
    matches = expert_ids[:, :, None] == expert_range
    picked = jnp.sum(jnp.where(matches, sigmoid_score[:, None, :], 0.0), axis=2)
    gates = picked / jnp.sum(picked, axis=1, keepdims=True)
    flat_ids = expert_ids.reshape(-1)
    one_hot = (flat_ids[:, None] == expert_range).astype(jnp.int32)
    slot_index = jnp.sum((jnp.cumsum(one_hot, axis=0) - one_hot) * one_hot, axis=1)
    target = flat_ids * capacity + slot_index
    token_of = jnp.arange(token_count * top_count, dtype=jnp.int32) // top_count
    source_row = (
        jnp.full((expert_count * capacity,), token_count, jnp.int32).at[target].set(token_of)
    )
    padded = jnp.concatenate([sent_rows, jnp.zeros((1, sent_rows.shape[1]), jnp.bfloat16)], axis=0)
    outgoing = padded[source_row].reshape(expert_count, capacity, sent_rows.shape[1])
    returned = run_rows(
        lax.all_to_all(outgoing, "ctx", split_axis=0, concat_axis=0, tiled=True),
        w_gate,
        w_up,
        w_down,
    )
    back_width = returned.shape[2]
    flat_back = returned.reshape(expert_count * capacity, back_width)
    slot_rows = target.reshape(token_count, top_count)
    moe_part = jnp.zeros((token_count, back_width), jnp.float32)
    for choice_number in range(top_count):
        picked_rows = flat_back[slot_rows[:, choice_number]].astype(jnp.float32)
        moe_part = moe_part + gates[:, choice_number][:, None] * picked_rows
    moe_sum = lax.psum_scatter(
        moe_part.astype(jnp.bfloat16), "exp", scatter_dimension=1, tiled=True
    ).astype(jnp.float32)
    return (hidden_own.astype(jnp.float32) + moe_sum).astype(jnp.bfloat16)


def solution(mesh):
    in_specs = (
        P("ctx", "exp"),
        P("ctx", "exp"),
        P("ctx", "exp"),
        P("ctx", "exp"),
        P("exp", "ctx"),
        P("exp"),
        P("exp"),
        P("exp", None),
        P("ctx", "exp"),
        P(),
        P(),
        P("ctx", None),
        P("ctx", "exp", None),
        P("ctx", "exp", None),
        P("ctx", "exp", None),
    )
    out_specs = P("ctx", "exp")
    return jax.shard_map(
        per_device, mesh=mesh, in_specs=in_specs, out_specs=out_specs, check_vma=False
    )
```

```python
import functools

import jax
import jax.numpy as jnp
from jax import lax
from jax.experimental import pallas as pl
from jax.experimental.pallas import tpu as pltpu
from jax.sharding import PartitionSpec as P

P_SIZE = 64
N = 128
PLANE = 4


def move(value, partner):
    return lax.ppermute(value, "ctx", [(i, partner(i)) for i in range(lax.axis_size("ctx"))])


def as_rows(flat, width):
    tile = 8 * width
    return jnp.pad(flat, (0, -flat.shape[0] % tile)).reshape(-1, width)


def chain_kernel(pairs, out):
    count, share, width = out.shape
    line = lax.broadcasted_iota(jnp.int32, (share, width), 0)
    lane = lax.broadcasted_iota(jnp.int32, (share, width), 1)
    entering = jnp.zeros((share, width), jnp.float32)
    for pair in range(count):
        out[pair] = entering
        logs = jnp.where(line == lane, pairs[pair, share : share + 1, :], 0.0)
        decay = jnp.exp(jnp.sum(logs, axis=1, keepdims=True))
        entering = decay * entering + pairs[pair, :share]


def prefix_states(state, log_total, extra, beside):
    size = lax.axis_size("ctx")
    odd = lax.axis_index("ctx") % 2 == 1
    rows, width = state.shape
    half = rows // 2
    share = rows // size
    extra_rows = extra.shape[0]
    row_log = jnp.repeat(log_total, rows // log_total.shape[0])

    def halves(array):
        return array[:half], array[half:]

    def pick(flag, first, second):
        return jnp.where(flag, second, first)

    low, high = halves(state)
    log_low, log_high = halves(row_log)
    kept, given = pick(odd, low, high), pick(odd, high, low)
    kept_log, given_log = pick(odd, log_low, log_high), pick(odd, log_high, log_low)
    log_rows = as_rows(given_log, width)
    got = move(jnp.concatenate([given, log_rows, extra], axis=0), lambda i: i ^ 1)
    got_log = got[half : half + log_rows.shape[0]].reshape(-1)[:half]
    got_extra = got[half + log_rows.shape[0] :]
    got = got[:half]
    first, second = pick(odd, kept, got), pick(odd, got, kept)
    first_log, second_log = pick(odd, kept_log, got_log), pick(odd, got_log, kept_log)
    pair_extra = jnp.concatenate([pick(odd, extra, got_extra), pick(odd, got_extra, extra)], axis=0)
    pair_state = jnp.exp(second_log)[:, None] * first + second
    pair_log = (first_log + second_log).reshape(size // 2, 1, share)
    pair_log = jnp.pad(pair_log, ((0, 0), (0, 7), (0, width - share)))
    pair_extra = jnp.broadcast_to(pair_extra[None], (size // 2, 2 * extra_rows, width))
    sent = jnp.concatenate(
        [pair_state.reshape(size // 2, share, width), pair_log, pair_extra], axis=1
    )
    groups = [[i for i in range(size) if i % 2 == k] for k in range(2)]

    def exchange(array):
        return lax.all_to_all(
            array, "ctx", split_axis=0, concat_axis=0, axis_index_groups=groups, tiled=True
        )

    pairs = exchange(sent)
    found = pl.pallas_call(
        chain_kernel, out_shape=jax.ShapeDtypeStruct((size // 2, share, width), jnp.float32)
    )(pairs)
    into_first = exchange(found).reshape(half, width)
    into_first, beside = lax.optimization_barrier((into_first, beside))
    into_second = jnp.exp(first_log)[:, None] * into_first + first
    back = move(pick(odd, into_second, into_first), lambda i: i ^ 1)
    into_first, first, first_log = lax.optimization_barrier((into_first, first, first_log))
    mine = pick(odd, into_first, jnp.exp(first_log)[:, None] * into_first + first)
    return mine, back, beside, pairs[:, share + 8 :].reshape(size, extra_rows, width)


def expert_kernel(planes, top, place, *refs):
    sources, refs = refs[: 4 * planes], refs[4 * planes :]
    ids, moe_gain, router, hbm_weights, refs = refs[0], refs[1], refs[2], refs[3:9], refs[9:]
    hbm_outs, refs = refs[: 4 * planes], refs[4 * planes :]
    rows, acts, weights, loaded = refs
    pieces, outs = sources, hbm_outs
    units = weights.shape[1]
    loads = [
        pltpu.make_async_copy(
            hbm_weights[i].at[pl.ds(part * units // 2, units // 2)],
            weights.at[i, pl.ds(part * units // 2, units // 2)],
            loaded.at[2 * i + part],
        )
        for i in (0, 1, 3, 4, 2, 5)
        for part in range(2)
    ]
    for copy in loads[:6]:
        copy.start()

    def load(index):
        for part in range(2 * index, 2 * index + 2):
            loads[part].wait()
            if part + 6 < len(loads):
                loads[part + 6].start()

    count, half = sources[0].shape
    width = 2 * half
    own = pl.multiple_of(place[1] * half, half)
    rest = pl.multiple_of((1 - place[1]) * half, half)
    gain_own, gain_rest = moe_gain[:, pl.ds(own, half)], moe_gain[:, pl.ds(rest, half)]
    contract = (((1,), (1,)), ((), ()))
    for plane in range(planes):
        for line in range(2):
            left = pieces[4 * plane + 2 * line][...].astype(jnp.float32)
            right = pieces[4 * plane + 2 * line + 1][...].astype(jnp.float32)
            total = jnp.sum(left * left, axis=1, keepdims=True) + jnp.sum(
                right * right, axis=1, keepdims=True
            )
            scale = lax.rsqrt(total / width + 1e-06)
            where = pl.ds((2 * plane + line) * count, count)
            rows[where, pl.ds(own, half)] = (left * scale * gain_own).astype(jnp.bfloat16)
            rows[where, pl.ds(rest, half)] = (right * scale * gain_rest).astype(jnp.bfloat16)

    logits = lax.dot_general(
        router[...], rows[...], (((0,), (1,)), ((), ())), preferred_element_type=jnp.float32
    )
    score = jax.nn.sigmoid(logits)
    experts = score.shape[0]
    number = lax.broadcasted_iota(jnp.int32, (experts, count), 0).astype(jnp.float32)
    shares = []
    for block in range(2 * planes):
        chosen = number == ids[block, 0:1, :]
        for choice in range(1, top):
            chosen = chosen | (number == ids[block, choice : choice + 1, :])
        picked = jnp.where(chosen, score[:, block * count : (block + 1) * count], 0.0)
        shares.append(picked / jnp.sum(picked, axis=0, keepdims=True))
    line = lax.broadcasted_iota(jnp.int32, (count, count), 0)
    lane = lax.broadcasted_iota(jnp.int32, (count, count), 1)
    expert = lax.broadcasted_iota(jnp.int32, (experts, count), 0)
    for which in range(2):
        columns = []
        for share in shares:
            row = jnp.sum(
                jnp.where(expert == place[2 * which], share, 0.0), axis=0, keepdims=True
            )
            columns.append(jnp.sum(jnp.where(line == lane, row, 0.0), axis=1, keepdims=True))
        gate = jnp.concatenate(columns, axis=0)
        load(2 * which)
        gate_proj = lax.dot_general(
            rows[...], weights[3 * which], contract, preferred_element_type=jnp.float32
        )
        load(2 * which + 1)
        up_proj = lax.dot_general(
            rows[...], weights[3 * which + 1], contract, preferred_element_type=jnp.float32
        )
        active = gate_proj / (1.0 + jnp.exp(-gate_proj)) * up_proj
        acts[which] = (active * gate).astype(jnp.bfloat16)
    load(4)
    load(5)
    for side, start in ((1, rest), (0, own)):
        part = jnp.dot(acts[0], weights[2, :, pl.ds(start, half)], preferred_element_type=jnp.float32)
        part += jnp.dot(
            acts[1], weights[5, :, pl.ds(start, half)], preferred_element_type=jnp.float32
        )
        part = part.astype(jnp.bfloat16)
        for plane in range(planes):
            for line in (1, 0):
                index = 4 * plane + 2 * line + side
                first = (2 * plane + line) * count
                outs[index][...] = part[first : first + count]


def run_expert(place, pieces, ids, top, moe_gain, router, weights):
    count, half = pieces[0].shape
    planes = len(pieces) // 4
    units, width = weights[0].shape
    rows = 2 * planes * count
    vmem = pl.BlockSpec(memory_space=pltpu.VMEM)
    return pl.pallas_call(
        functools.partial(expert_kernel, planes, top),
        out_shape=[jax.ShapeDtypeStruct((count, half), jnp.bfloat16)] * (4 * planes),
        in_specs=[pl.BlockSpec(memory_space=pltpu.SMEM)]
        + [vmem] * (4 * planes)
        + [vmem] * 3
        + [pl.BlockSpec(memory_space=pltpu.HBM)] * 6,
        out_specs=[vmem] * (4 * planes),
        scratch_shapes=[
            pltpu.VMEM((rows, width), jnp.bfloat16),
            pltpu.VMEM((2, rows, units), jnp.bfloat16),
            pltpu.VMEM((6, units, width), jnp.bfloat16),
            pltpu.SemaphoreType.DMA((12,)),
        ],
        compiler_params=pltpu.CompilerParams(vmem_limit_bytes=56 * 2**20),
        cost_estimate=pl.CostEstimate(
            flops=2 * 6 * rows * width * units,
            bytes_accessed=2 * (6 * units * width + 8 * planes * count * half),
            transcendentals=2 * rows * units,
        ),
    )(place, *pieces, ids, moe_gain, router, *weights)


def dense_experts(place, hidden, every_ids, top, moe_gain, router, weights):
    size = lax.axis_size("ctx")
    planes = size // PLANE
    here = lax.axis_index("ctx")
    even = here % 2 == 0

    def flip(value, bit):
        return move(value, lambda i: i ^ bit)

    def across(value):
        return lax.ppermute(value, "exp", [(0, 1), (1, 0)])

    def diagonal(value):
        pairs = [
            (i * 2 + x, i * 2 + 1 - x if i % 2 == 0 else (i ^ 2) * 2 + x)
            for i in range(size)
            for x in range(2)
        ]
        return lax.ppermute(value, ("ctx", "exp"), pairs)

    def shift(value, planes_on):
        return move(value, lambda i: (i + PLANE * planes_on) % size)

    weights = [*weights, *(flip(weight, 1) for weight in weights)]
    groups = [[0],[1],[2],[3]]
    phases = [
        [("x", 0), ("y", 0)],
        [("diag", 0), ("z", 1)],
        [("K", 0), ("x", 1), ("y", 1), ("z", 2)],
        [("diag", 1), ("x", 2), ("y", 2), ("z", 3)],
        [("K", 1), ("x", 3), ("y", 3), ("diag", 2), ("rdiag", 0)],
        [("K", 2), ("diag", 3), ("rx", 0), ("ry", 0), ("rdiag", 1)],
        [("K", 3), ("rx", 1), ("ry", 1), ("rdiag", 2)],
        [("rx", 2), ("ry", 2), ("rdiag", 3), ("rz", 1)],
        [("rx", 3), ("ry", 3), ("rz", 2)],
        [("rz", 3)],
    ]
    done = {("z", 0): hidden}

    def operands(name, p):
        if name == "z":
            return [done["z", 0]]
        if name in ("x", "y"):
            return [done["z", p]]
        if name == "diag":
            return [jnp.where(even, done["y", p], done["x", p])]
        if name == "K":
            return [done[part, q] for q in groups[p] for part in ("z", "x", "y", "diag")]
        group = [g for g in range(len(groups)) if p in groups[g]][0]
        kept, to_x, to_y, corner = done["K", group][4 * groups[group].index(p) :][:4]
        if name == "rdiag":
            return [corner]
        zero = jnp.zeros_like(corner)
        if name == "rx":
            return [to_x + jnp.where(even, zero, done["rdiag", p])]
        if name == "ry":
            return [to_y + jnp.where(even, done["rdiag", p], zero)]
        parts = (kept, done["rx", p], done["ry", p])
        return [sum(part.astype(jnp.float32) for part in parts).astype(jnp.bfloat16)]

    def run(name, p, values):
        if name in ("z", "rz"):
            return [shift(values[0], -p if name == "z" else p)]
        if name in ("x", "rx"):
            return [across(values[0])]
        if name in ("y", "ry"):
            return [flip(values[0], 2)]
        if name in ("diag", "rdiag"):
            return [diagonal(values[0])]
        order = jnp.stack(
            [
                (here // PLANE + plane) % planes * PLANE + ((here % PLANE) ^ flips)
                for plane in groups[p]
                for flips in (0, 2)
            ]
        )
        return run_expert(place, values, every_ids[order], top, moe_gain[None], router, weights)

    for phase in phases:
        outs = [run(*step, operands(*step)) for step in phase]
        flat = [value for values in outs for value in values]
        held = list(lax.optimization_barrier((done["z", 0], *flat)))
        done["z", 0] = held.pop(0)
        for step, values in zip(phase, outs):
            values = [held.pop(0) for _ in values]
            done[step] = values if step[0] == "K" else values[0]
    total = hidden.astype(jnp.float32)
    group = [g for g in range(len(groups)) if 0 in groups[g]][0]
    total = total + done["K", group][4 * groups[group].index(0)].astype(jnp.float32)
    total = total + done["rx", 0].astype(jnp.float32) + done["ry", 0].astype(jnp.float32)
    for plane in range(1, planes):
        total = total + done["rz", plane].astype(jnp.float32)
    return total.astype(jnp.bfloat16)


def run_rows(pieces, w_gate, w_up, w_down):
    row_count = pieces.shape[0] * pieces.shape[1]
    flattened = pieces.reshape(row_count, pieces.shape[2])
    contract = (((1,), (1,)), ((), ()))
    gate_proj = lax.dot_general(flattened, w_gate[0], contract, preferred_element_type=jnp.float32)
    up_proj = lax.dot_general(flattened, w_up[0], contract, preferred_element_type=jnp.float32)
    active = (jax.nn.silu(gate_proj) * up_proj).astype(jnp.bfloat16)
    partial_value = jnp.dot(active, w_down[0], preferred_element_type=jnp.float32).astype(
        jnp.bfloat16
    )
    full_width = partial_value.shape[1]
    shaped = partial_value.reshape(pieces.shape[0], pieces.shape[1], full_width)
    return lax.all_to_all(shaped, "ctx", split_axis=0, concat_axis=0, tiled=True)


def columns_of(rows):
    pad = jnp.zeros((-rows.shape[0] % 128, rows.shape[1]), rows.dtype)
    return jnp.concatenate([rows, pad], axis=0).T if pad.shape[0] else rows.T


def column_of(row):
    size = row.shape[1]
    line = lax.broadcasted_iota(jnp.int32, (size, size), 0)
    lane = lax.broadcasted_iota(jnp.int32, (size, size), 1)
    return jnp.sum(jnp.where(line == lane, row, 0.0), axis=1, keepdims=True)


def state_kernel(rate, step_hbm, x_hbm, b_hbm, state, running, step, x, b, came):
    copies = [
        pltpu.make_async_copy(source, target, came.at[i])
        for i, (source, target) in enumerate(((step_hbm, step), (x_hbm, x), (b_hbm, b)))
    ]
    for copy in copies:
        copy.start()
    heads, count = step.shape
    groups = b.shape[1] // N
    per_group = heads // groups
    wide = per_group * P_SIZE
    copies[0].wait()
    total = -step[...] * column_of(rate[...])
    lane = lax.broadcasted_iota(jnp.int32, (heads, count), 1)
    hop = 1
    while hop < count:
        total = total + jnp.where(lane >= hop, pltpu.roll(total, hop, 1), 0.0)
        hop *= 2
    running[...] = total
    weight = jnp.exp(total[:, count - 1 :] - total) * step[...]
    copies[1].wait()
    copies[2].wait()
    for group in range(groups):
        turned = x[:, group * wide : (group + 1) * wide].astype(jnp.float32).T
        carried = jnp.concatenate(
            [
                turned[q * P_SIZE : (q + 1) * P_SIZE]
                * weight[group * per_group + q : group * per_group + q + 1]
                for q in range(per_group)
            ],
            axis=0,
        ).astype(jnp.bfloat16)
        state[group * wide : (group + 1) * wide] = jnp.dot(
            carried, b[:, group * N : (group + 1) * N], preferred_element_type=jnp.float32
        )


def inner_kernel(step, running, x, b, c, inner):
    heads, count = step.shape
    groups = b.shape[1] // N
    per_group = heads // groups
    total = running[...]
    columns = columns_of(total)
    line = lax.broadcasted_iota(jnp.int32, (count, count), 0)
    lane = lax.broadcasted_iota(jnp.int32, (count, count), 1)
    first = lax.broadcasted_iota(jnp.int32, (count, 2 * P_SIZE), 1) < P_SIZE
    for group in range(groups):
        where = slice(group * N, (group + 1) * N)
        scores = lax.dot_general(
            c[:, where], b[:, where], (((1,), (1,)), ((), ())), preferred_element_type=jnp.float32
        )
        scores = jnp.where(line >= lane, scores, 0.0)
        for pair in range(per_group // 2):
            head = group * per_group + 2 * pair
            mixing = []
            for h in (head, head + 1):
                spread = columns[:, h : h + 1] - total[h : h + 1]
                decay = jnp.exp(jnp.where(line >= lane, spread, 0.0))
                mixing.append((decay * scores * step[h : h + 1]).astype(jnp.bfloat16))
            both = x[:, head * P_SIZE : (head + 2) * P_SIZE].astype(jnp.float32)
            apart = jnp.concatenate(
                [jnp.where(first, both, 0.0), jnp.where(first, 0.0, both)], axis=0
            )
            inner[:, head * P_SIZE : (head + 2) * P_SIZE] = jnp.dot(
                jnp.concatenate(mixing, axis=1),
                apart.astype(jnp.bfloat16),
                preferred_element_type=jnp.float32,
            )


def project(place, rows, weight_hbm, weight, came, first, last, give):
    shares, _, width = weight.shape
    total = weight_hbm.shape[1] // width
    copies = []
    for step in range(first, last):
        start = pl.multiple_of(lax.rem(place[1] + step, total) * width, width)
        copies.append(
            pltpu.make_async_copy(
                weight_hbm.at[:, pl.ds(start, width)], weight.at[step - first], came.at[step - first]
            )
        )
    yield [copy.start() for copy in copies]
    for step in range(first, last):
        copies[step - first].wait()
        give(
            step,
            jnp.dot(rows[...], weight[step - first], preferred_element_type=jnp.float32),
        )
    yield


def own_kernel(place, normed, weight_hbm, stream, own, weight, came):
    def give(step, part):
        own[...] = part + stream[...].astype(jnp.float32)

    for _ in project(place, normed, weight_hbm, weight, came, 0, 1, give):
        pass


def mixer_kernel(place, weight_hbm, *refs):
    sources, (normed, theirs), refs = refs[:7], refs[7:9], refs[9:]
    targets, (high, low, weight, came, fetched) = refs[:7], refs[7:]
    fetches = [
        pltpu.make_async_copy(source, target, fetched.at[i])
        for i, (source, target) in enumerate(zip(sources, targets))
    ]
    for fetch in fetches:
        fetch.start()
    inner, running, c, z, mine, back, gain = targets

    def give(step, part):
        theirs[step - 1] = part.astype(jnp.bfloat16)

    projection = project(
        place, normed, weight_hbm, weight, came, 1, theirs.shape[0] + 1, give
    )
    next(projection)
    for fetch in fetches:
        fetch.wait()
    heads, count = running.shape
    groups = c.shape[1] // N
    per_group = heads // groups
    wide = per_group * P_SIZE
    half = mine.shape[0]
    odd = place[0] % 2
    for part in range(2):
        value = jnp.where(odd == part, mine[...], back[...])
        rounded = value.astype(jnp.bfloat16)
        high[part * half : (part + 1) * half] = rounded
        low[part * half : (part + 1) * half] = (value - rounded.astype(jnp.float32)).astype(
            jnp.bfloat16
        )
    growth = columns_of(jnp.exp(running[...]))
    first = lax.broadcasted_iota(jnp.int32, (count, 2 * P_SIZE), 1) < P_SIZE
    contract = (((1,), (1,)), ((), ()))
    for group in range(groups):
        where = slice(group * wide, (group + 1) * wide)
        reads = c[:, group * N : (group + 1) * N]
        carried = lax.dot_general(
            reads, high[where], contract, preferred_element_type=jnp.float32
        ) + lax.dot_general(reads, low[where], contract, preferred_element_type=jnp.float32)
        heads_in = range(group * per_group, (group + 1) * per_group, 2)
        scale = jnp.concatenate(
            [jnp.where(first, growth[:, h : h + 1], growth[:, h + 1 : h + 2]) for h in heads_in],
            axis=1,
        )
        gate = z[:, where].astype(jnp.float32)
        gated = (inner[:, where] + scale * carried) * (gate / (1.0 + jnp.exp(-gate)))
        mean = jnp.sum(gated * gated, axis=1, keepdims=True) / wide
        normed[:, where] = (gated * lax.rsqrt(mean + 1e-05) * gain[:, where]).astype(jnp.bfloat16)
    next(projection)


def per_device(
    ssm_input,
    gate_input,
    b_input,
    c_input,
    step_size,
    decay_rate,
    norm_gain,
    out_weight,
    stream,
    moe_gain,
    router,
    expert_ids,
    w_gate,
    w_up,
    w_down,
):
    token_count, inner_width = ssm_input.shape
    head_count = step_size.shape[0]
    slice_width = stream.shape[1]
    expert_count = router.shape[1]
    top_count = expert_ids.shape[1]
    exp_size = lax.axis_size("exp")
    capacity = max(
        2, token_count * top_count // expert_count + token_count * top_count // (4 * expert_count)
    )
    vmem = pl.BlockSpec(memory_space=pltpu.VMEM)
    hbm = pl.BlockSpec(memory_space=pltpu.HBM)
    state, running = pl.pallas_call(
        state_kernel,
        out_shape=[
            jax.ShapeDtypeStruct((inner_width, N), jnp.float32),
            jax.ShapeDtypeStruct(step_size.shape, jnp.float32),
        ],
        in_specs=[vmem] + [hbm] * 3,
        out_specs=[vmem] * 2,
        scratch_shapes=[
            pltpu.VMEM(step_size.shape, jnp.float32),
            pltpu.VMEM(ssm_input.shape, jnp.bfloat16),
            pltpu.VMEM(b_input.shape, jnp.bfloat16),
            pltpu.SemaphoreType.DMA((3,)),
        ],
        compiler_params=pltpu.CompilerParams(vmem_limit_bytes=16 * 2**20),
    )(decay_rate[None], step_size, ssm_input, b_input)
    id_rows = jnp.pad(expert_ids.T.astype(jnp.float32), ((0, -expert_ids.shape[1] % 8), (0, 0)))
    inner = pl.pallas_call(
        inner_kernel,
        out_shape=jax.ShapeDtypeStruct((token_count, inner_width), jnp.float32),
        in_specs=[vmem] * 5,
        out_specs=vmem,
        compiler_params=pltpu.CompilerParams(vmem_limit_bytes=16 * 2**20),
        cost_estimate=pl.CostEstimate(
            flops=4 * inner_width * token_count * token_count,
            bytes_accessed=8 * inner_width * token_count,
            transcendentals=head_count * token_count * token_count,
        ),
    )(step_size, running, ssm_input, b_input, c_input)
    mine, back, inner, every_ids = prefix_states(state, running[:, -1], id_rows, inner)
    here = lax.axis_index("ctx")
    place = jnp.stack([here, lax.axis_index("exp"), here ^ 1]).astype(jnp.int32)
    fetched = (
        inner,
        running,
        c_input,
        gate_input,
        mine,
        back,
        norm_gain[None],
    )
    normed, theirs = pl.pallas_call(
        mixer_kernel,
        out_shape=[
            jax.ShapeDtypeStruct((token_count, inner_width), jnp.bfloat16),
            jax.ShapeDtypeStruct((exp_size - 1, *stream.shape), jnp.bfloat16),
        ],
        in_specs=[pl.BlockSpec(memory_space=pltpu.SMEM)] + [hbm] * 8,
        out_specs=[vmem] * 2,
        scratch_shapes=[pltpu.VMEM(array.shape, array.dtype) for array in fetched]
        + [
            pltpu.VMEM((inner_width, N), jnp.bfloat16),
            pltpu.VMEM((inner_width, N), jnp.bfloat16),
            pltpu.VMEM((exp_size - 1, inner_width, slice_width), jnp.bfloat16),
            pltpu.SemaphoreType.DMA((exp_size - 1,)),
            pltpu.SemaphoreType.DMA((7,)),
        ],
        compiler_params=pltpu.CompilerParams(vmem_limit_bytes=60 * 2**20),
    )(place, out_weight, *fetched)
    hidden_own = pl.pallas_call(
        own_kernel,
        out_shape=jax.ShapeDtypeStruct(stream.shape, jnp.float32),
        in_specs=[pl.BlockSpec(memory_space=pltpu.SMEM), vmem, hbm, vmem],
        out_specs=vmem,
        scratch_shapes=[
            pltpu.VMEM((1, inner_width, slice_width), jnp.bfloat16),
            pltpu.SemaphoreType.DMA((1,)),
        ],
        compiler_params=pltpu.CompilerParams(vmem_limit_bytes=60 * 2**20),
        cost_estimate=pl.CostEstimate(
            flops=2 * token_count * inner_width * slice_width,
            bytes_accessed=2 * inner_width * slice_width,
            transcendentals=0,
        ),
    )(place, normed, out_weight, stream)
    for step in range(1, exp_size):
        ring = [(i, (i + step) % exp_size) for i in range(exp_size)]
        sent = lax.ppermute(theirs[step - 1], "exp", ring)
        hidden_own = hidden_own + sent.astype(jnp.float32)
    hidden_own = hidden_own.astype(jnp.bfloat16)
    every_token = token_count * lax.axis_size("ctx")
    if exp_size == 2 and every_token <= 3 * expert_count * capacity:
        return dense_experts(
            place,
            hidden_own,
            every_ids,
            top_count,
            moe_gain,
            router,
            (w_gate[0], w_up[0], w_down[0]),
        )
    hidden_all = lax.all_gather(hidden_own, "exp", axis=1, tiled=True)
    hidden_f = hidden_all.astype(jnp.float32)
    mean_h = jnp.mean(hidden_f * hidden_f, axis=1, keepdims=True)
    sent_rows = (hidden_f * lax.rsqrt(mean_h + 1e-06) * moe_gain).astype(jnp.bfloat16)
    logits = jnp.dot(sent_rows, router, preferred_element_type=jnp.float32)
    sigmoid_score = jax.nn.sigmoid(logits)
    expert_range = jnp.arange(expert_count, dtype=jnp.int32)
    matches = expert_ids[:, :, None] == expert_range
    picked = jnp.sum(jnp.where(matches, sigmoid_score[:, None, :], 0.0), axis=2)
    gates = picked / jnp.sum(picked, axis=1, keepdims=True)
    flat_ids = expert_ids.reshape(-1)
    one_hot = (flat_ids[:, None] == expert_range).astype(jnp.int32)
    slot_index = jnp.sum((jnp.cumsum(one_hot, axis=0) - one_hot) * one_hot, axis=1)
    target = flat_ids * capacity + slot_index
    token_of = jnp.arange(token_count * top_count, dtype=jnp.int32) // top_count
    source_row = (
        jnp.full((expert_count * capacity,), token_count, jnp.int32).at[target].set(token_of)
    )
    padded = jnp.concatenate([sent_rows, jnp.zeros((1, sent_rows.shape[1]), jnp.bfloat16)], axis=0)
    outgoing = padded[source_row].reshape(expert_count, capacity, sent_rows.shape[1])
    returned = run_rows(
        lax.all_to_all(outgoing, "ctx", split_axis=0, concat_axis=0, tiled=True),
        w_gate,
        w_up,
        w_down,
    )
    back_width = returned.shape[2]
    flat_back = returned.reshape(expert_count * capacity, back_width)
    slot_rows = target.reshape(token_count, top_count)
    moe_part = jnp.zeros((token_count, back_width), jnp.float32)
    for choice_number in range(top_count):
        picked_rows = flat_back[slot_rows[:, choice_number]].astype(jnp.float32)
        moe_part = moe_part + gates[:, choice_number][:, None] * picked_rows
    moe_sum = lax.psum_scatter(
        moe_part.astype(jnp.bfloat16), "exp", scatter_dimension=1, tiled=True
    ).astype(jnp.float32)
    return (hidden_own.astype(jnp.float32) + moe_sum).astype(jnp.bfloat16)


def solution(mesh):
    in_specs = (
        P("ctx", "exp"),
        P("ctx", "exp"),
        P("ctx", "exp"),
        P("ctx", "exp"),
        P("exp", "ctx"),
        P("exp"),
        P("exp"),
        P("exp", None),
        P("ctx", "exp"),
        P(),
        P(),
        P("ctx", None),
        P("ctx", "exp", None),
        P("ctx", "exp", None),
        P("ctx", "exp", None),
    )
    out_specs = P("ctx", "exp")
    return jax.shard_map(
        per_device, mesh=mesh, in_specs=in_specs, out_specs=out_specs, check_vma=False
    )
```

```python
import functools

import jax
import jax.numpy as jnp
from jax import lax
from jax.experimental import pallas as pl
from jax.experimental.pallas import tpu as pltpu
from jax.sharding import PartitionSpec as P

P_SIZE = 64
N = 128
PLANE = 4


def move(value, partner):
    return lax.ppermute(value, "ctx", [(i, partner(i)) for i in range(lax.axis_size("ctx"))])


def as_rows(flat, width):
    tile = 8 * width
    return jnp.pad(flat, (0, -flat.shape[0] % tile)).reshape(-1, width)


def chain_kernel(pairs, out):
    count, share, width = out.shape
    line = lax.broadcasted_iota(jnp.int32, (share, width), 0)
    lane = lax.broadcasted_iota(jnp.int32, (share, width), 1)
    entering = jnp.zeros((share, width), jnp.float32)
    for pair in range(count):
        out[pair] = entering
        logs = jnp.where(line == lane, pairs[pair, share : share + 1, :], 0.0)
        decay = jnp.exp(jnp.sum(logs, axis=1, keepdims=True))
        entering = decay * entering + pairs[pair, :share]


def prefix_states(state, log_total, extra, beside):
    size = lax.axis_size("ctx")
    odd = lax.axis_index("ctx") % 2 == 1
    rows, width = state.shape
    half = rows // 2
    share = rows // size
    extra_rows = extra.shape[0]
    row_log = jnp.repeat(log_total, rows // log_total.shape[0])

    def halves(array):
        return array[:half], array[half:]

    def pick(flag, first, second):
        return jnp.where(flag, second, first)

    low, high = halves(state)
    log_low, log_high = halves(row_log)
    kept, given = pick(odd, low, high), pick(odd, high, low)
    kept_log, given_log = pick(odd, log_low, log_high), pick(odd, log_high, log_low)
    log_rows = as_rows(given_log, width)
    got = move(jnp.concatenate([given, log_rows, extra], axis=0), lambda i: i ^ 1)
    got_log = got[half : half + log_rows.shape[0]].reshape(-1)[:half]
    got_extra = got[half + log_rows.shape[0] :]
    got = got[:half]
    first, second = pick(odd, kept, got), pick(odd, got, kept)
    first_log, second_log = pick(odd, kept_log, got_log), pick(odd, got_log, kept_log)
    pair_extra = jnp.concatenate([pick(odd, extra, got_extra), pick(odd, got_extra, extra)], axis=0)
    pair_state = jnp.exp(second_log)[:, None] * first + second
    pair_log = (first_log + second_log).reshape(size // 2, 1, share)
    pair_log = jnp.pad(pair_log, ((0, 0), (0, 7), (0, width - share)))
    pair_extra = jnp.broadcast_to(pair_extra[None], (size // 2, 2 * extra_rows, width))
    sent = jnp.concatenate(
        [pair_state.reshape(size // 2, share, width), pair_log, pair_extra], axis=1
    )
    groups = [[i for i in range(size) if i % 2 == k] for k in range(2)]

    def exchange(array):
        return lax.all_to_all(
            array, "ctx", split_axis=0, concat_axis=0, axis_index_groups=groups, tiled=True
        )

    pairs = exchange(sent)
    found = pl.pallas_call(
        chain_kernel, out_shape=jax.ShapeDtypeStruct((size // 2, share, width), jnp.float32)
    )(pairs)
    into_first = exchange(found).reshape(half, width)
    into_first, *beside = lax.optimization_barrier((into_first, *beside))
    into_second = jnp.exp(first_log)[:, None] * into_first + first
    back = move(pick(odd, into_second, into_first), lambda i: i ^ 1)
    into_first, first, first_log = lax.optimization_barrier((into_first, first, first_log))
    mine = pick(odd, into_first, jnp.exp(first_log)[:, None] * into_first + first)
    return mine, back, beside, pairs[:, share + 8 :].reshape(size, extra_rows, width)


def expert_kernel(planes, top, place, *refs):
    sources, refs = refs[: 4 * planes], refs[4 * planes :]
    ids, moe_gain, router, hbm_weights, refs = refs[0], refs[1], refs[2], refs[3:9], refs[9:]
    hbm_outs, refs = refs[: 4 * planes], refs[4 * planes :]
    rows, acts, weights, loaded = refs
    pieces, outs = sources, hbm_outs
    units = weights.shape[1]
    loads = [
        pltpu.make_async_copy(
            hbm_weights[i].at[pl.ds(part * units // 2, units // 2)],
            weights.at[i, pl.ds(part * units // 2, units // 2)],
            loaded.at[2 * i + part],
        )
        for i in (0, 1, 3, 4, 2, 5)
        for part in range(2)
    ]
    for copy in loads[:6]:
        copy.start()

    def load(index):
        for part in range(2 * index, 2 * index + 2):
            loads[part].wait()
            if part + 6 < len(loads):
                loads[part + 6].start()

    count, half = sources[0].shape
    width = 2 * half
    own = pl.multiple_of(place[1] * half, half)
    rest = pl.multiple_of((1 - place[1]) * half, half)
    gain_own, gain_rest = moe_gain[:, pl.ds(own, half)], moe_gain[:, pl.ds(rest, half)]
    contract = (((1,), (1,)), ((), ()))
    for plane in range(planes):
        for line in range(2):
            left = pieces[4 * plane + 2 * line][...].astype(jnp.float32)
            right = pieces[4 * plane + 2 * line + 1][...].astype(jnp.float32)
            total = jnp.sum(left * left, axis=1, keepdims=True) + jnp.sum(
                right * right, axis=1, keepdims=True
            )
            scale = lax.rsqrt(total / width + 1e-06)
            where = pl.ds((2 * plane + line) * count, count)
            rows[where, pl.ds(own, half)] = (left * scale * gain_own).astype(jnp.bfloat16)
            rows[where, pl.ds(rest, half)] = (right * scale * gain_rest).astype(jnp.bfloat16)

    logits = lax.dot_general(
        router[...], rows[...], (((0,), (1,)), ((), ())), preferred_element_type=jnp.float32
    )
    score = jax.nn.sigmoid(logits)
    experts = score.shape[0]
    number = lax.broadcasted_iota(jnp.int32, (experts, count), 0).astype(jnp.float32)
    shares = []
    for block in range(2 * planes):
        chosen = number == ids[block, 0:1, :]
        for choice in range(1, top):
            chosen = chosen | (number == ids[block, choice : choice + 1, :])
        picked = jnp.where(chosen, score[:, block * count : (block + 1) * count], 0.0)
        shares.append(picked / jnp.sum(picked, axis=0, keepdims=True))
    line = lax.broadcasted_iota(jnp.int32, (count, count), 0)
    lane = lax.broadcasted_iota(jnp.int32, (count, count), 1)
    expert = lax.broadcasted_iota(jnp.int32, (experts, count), 0)
    for which in range(2):
        columns = []
        for share in shares:
            row = jnp.sum(
                jnp.where(expert == place[2 * which], share, 0.0), axis=0, keepdims=True
            )
            columns.append(jnp.sum(jnp.where(line == lane, row, 0.0), axis=1, keepdims=True))
        gate = jnp.concatenate(columns, axis=0)
        load(2 * which)
        gate_proj = lax.dot_general(
            rows[...], weights[3 * which], contract, preferred_element_type=jnp.float32
        )
        load(2 * which + 1)
        up_proj = lax.dot_general(
            rows[...], weights[3 * which + 1], contract, preferred_element_type=jnp.float32
        )
        active = gate_proj / (1.0 + jnp.exp(-gate_proj)) * up_proj
        acts[which] = (active * gate).astype(jnp.bfloat16)
    load(4)
    load(5)
    for side, start in ((1, rest), (0, own)):
        part = jnp.dot(acts[0], weights[2, :, pl.ds(start, half)], preferred_element_type=jnp.float32)
        part += jnp.dot(
            acts[1], weights[5, :, pl.ds(start, half)], preferred_element_type=jnp.float32
        )
        part = part.astype(jnp.bfloat16)
        for plane in range(planes):
            for line in (1, 0):
                index = 4 * plane + 2 * line + side
                first = (2 * plane + line) * count
                outs[index][...] = part[first : first + count]


def run_expert(place, pieces, ids, top, moe_gain, router, weights):
    count, half = pieces[0].shape
    planes = len(pieces) // 4
    units, width = weights[0].shape
    rows = 2 * planes * count
    vmem = pl.BlockSpec(memory_space=pltpu.VMEM)
    return pl.pallas_call(
        functools.partial(expert_kernel, planes, top),
        out_shape=[jax.ShapeDtypeStruct((count, half), jnp.bfloat16)] * (4 * planes),
        in_specs=[pl.BlockSpec(memory_space=pltpu.SMEM)]
        + [vmem] * (4 * planes)
        + [vmem] * 3
        + [pl.BlockSpec(memory_space=pltpu.HBM)] * 6,
        out_specs=[vmem] * (4 * planes),
        scratch_shapes=[
            pltpu.VMEM((rows, width), jnp.bfloat16),
            pltpu.VMEM((2, rows, units), jnp.bfloat16),
            pltpu.VMEM((6, units, width), jnp.bfloat16),
            pltpu.SemaphoreType.DMA((12,)),
        ],
        compiler_params=pltpu.CompilerParams(vmem_limit_bytes=56 * 2**20),
        cost_estimate=pl.CostEstimate(
            flops=2 * 6 * rows * width * units,
            bytes_accessed=2 * (6 * units * width + 8 * planes * count * half),
            transcendentals=2 * rows * units,
        ),
    )(place, *pieces, ids, moe_gain, router, *weights)


def dense_experts(place, hidden, every_ids, top, moe_gain, router, weights):
    size = lax.axis_size("ctx")
    planes = size // PLANE
    here = lax.axis_index("ctx")
    even = here % 2 == 0

    def flip(value, bit):
        return move(value, lambda i: i ^ bit)

    def across(value):
        return lax.ppermute(value, "exp", [(0, 1), (1, 0)])

    def diagonal(value):
        pairs = [
            (i * 2 + x, i * 2 + 1 - x if i % 2 == 0 else (i ^ 2) * 2 + x)
            for i in range(size)
            for x in range(2)
        ]
        return lax.ppermute(value, ("ctx", "exp"), pairs)

    def shift(value, planes_on):
        return move(value, lambda i: (i + PLANE * planes_on) % size)

    weights = [*weights, *(flip(weight, 1) for weight in weights)]
    groups = [[0],[1],[2],[3]]
    phases = [
        [("x", 0), ("y", 0)],
        [("diag", 0), ("z", 1)],
        [("K", 0), ("x", 1), ("y", 1), ("z", 2)],
        [("diag", 1), ("x", 2), ("y", 2), ("z", 3)],
        [("K", 1), ("x", 3), ("y", 3), ("diag", 2)],
        [("K", 2), ("diag", 3), ("rdiag", 0), ("rdiag", 1)],
        [("K", 3), ("rx", 0), ("ry", 0), ("rx", 1), ("ry", 1), ("rdiag", 2)],
        [("rx", 2), ("ry", 2), ("rdiag", 3), ("rz", 1)],
        [("rx", 3), ("ry", 3), ("rz", 2)],
        [("rz", 3)],
    ]
    done = {("z", 0): hidden}

    def operands(name, p):
        if name == "z":
            return [done["z", 0]]
        if name in ("x", "y"):
            return [done["z", p]]
        if name == "diag":
            return [jnp.where(even, done["y", p], done["x", p])]
        if name == "K":
            return [done[part, q] for q in groups[p] for part in ("z", "x", "y", "diag")]
        group = [g for g in range(len(groups)) if p in groups[g]][0]
        kept, to_x, to_y, corner = done["K", group][4 * groups[group].index(p) :][:4]
        if name == "rdiag":
            return [corner]
        zero = jnp.zeros_like(corner)
        if name == "rx":
            return [to_x + jnp.where(even, zero, done["rdiag", p])]
        if name == "ry":
            return [to_y + jnp.where(even, done["rdiag", p], zero)]
        parts = (kept, done["rx", p], done["ry", p])
        return [sum(part.astype(jnp.float32) for part in parts).astype(jnp.bfloat16)]

    def run(name, p, values):
        if name in ("z", "rz"):
            return [shift(values[0], -p if name == "z" else p)]
        if name in ("x", "rx"):
            return [across(values[0])]
        if name in ("y", "ry"):
            return [flip(values[0], 2)]
        if name in ("diag", "rdiag"):
            return [diagonal(values[0])]
        order = jnp.stack(
            [
                (here // PLANE + plane) % planes * PLANE + ((here % PLANE) ^ flips)
                for plane in groups[p]
                for flips in (0, 2)
            ]
        )
        return run_expert(place, values, every_ids[order], top, moe_gain, router, weights)

    for phase in phases:
        outs = [run(*step, operands(*step)) for step in phase]
        flat = [value for values in outs for value in values]
        held = list(lax.optimization_barrier((done["z", 0], *flat)))
        done["z", 0] = held.pop(0)
        for step, values in zip(phase, outs):
            values = [held.pop(0) for _ in values]
            done[step] = values if step[0] == "K" else values[0]
    total = hidden.astype(jnp.float32)
    group = [g for g in range(len(groups)) if 0 in groups[g]][0]
    total = total + done["K", group][4 * groups[group].index(0)].astype(jnp.float32)
    total = total + done["rx", 0].astype(jnp.float32) + done["ry", 0].astype(jnp.float32)
    for plane in range(1, planes):
        total = total + done["rz", plane].astype(jnp.float32)
    return total.astype(jnp.bfloat16)


def run_rows(pieces, w_gate, w_up, w_down):
    row_count = pieces.shape[0] * pieces.shape[1]
    flattened = pieces.reshape(row_count, pieces.shape[2])
    contract = (((1,), (1,)), ((), ()))
    gate_proj = lax.dot_general(flattened, w_gate[0], contract, preferred_element_type=jnp.float32)
    up_proj = lax.dot_general(flattened, w_up[0], contract, preferred_element_type=jnp.float32)
    active = (jax.nn.silu(gate_proj) * up_proj).astype(jnp.bfloat16)
    partial_value = jnp.dot(active, w_down[0], preferred_element_type=jnp.float32).astype(
        jnp.bfloat16
    )
    full_width = partial_value.shape[1]
    shaped = partial_value.reshape(pieces.shape[0], pieces.shape[1], full_width)
    return lax.all_to_all(shaped, "ctx", split_axis=0, concat_axis=0, tiled=True)


def columns_of(rows):
    pad = jnp.zeros((-rows.shape[0] % 128, rows.shape[1]), rows.dtype)
    return jnp.concatenate([rows, pad], axis=0).T if pad.shape[0] else rows.T


def column_of(row):
    size = row.shape[1]
    line = lax.broadcasted_iota(jnp.int32, (size, size), 0)
    lane = lax.broadcasted_iota(jnp.int32, (size, size), 1)
    return jnp.sum(jnp.where(line == lane, row, 0.0), axis=1, keepdims=True)


def state_kernel(rate, step_hbm, x_hbm, b_hbm, state, running, step, x, b, came):
    copies = [
        pltpu.make_async_copy(source, target, came.at[i])
        for i, (source, target) in enumerate(((step_hbm, step), (x_hbm, x), (b_hbm, b)))
    ]
    for copy in copies:
        copy.start()
    heads, count = step.shape
    groups = b.shape[1] // N
    per_group = heads // groups
    wide = per_group * P_SIZE
    copies[0].wait()
    total = -step[...] * column_of(rate[...])
    lane = lax.broadcasted_iota(jnp.int32, (heads, count), 1)
    hop = 1
    while hop < count:
        total = total + jnp.where(lane >= hop, pltpu.roll(total, hop, 1), 0.0)
        hop *= 2
    running[...] = total
    weight = jnp.exp(total[:, count - 1 :] - total) * step[...]
    copies[1].wait()
    copies[2].wait()
    for group in range(groups):
        turned = x[:, group * wide : (group + 1) * wide].astype(jnp.float32).T
        carried = jnp.concatenate(
            [
                turned[q * P_SIZE : (q + 1) * P_SIZE]
                * weight[group * per_group + q : group * per_group + q + 1]
                for q in range(per_group)
            ],
            axis=0,
        ).astype(jnp.bfloat16)
        state[group * wide : (group + 1) * wide] = jnp.dot(
            carried, b[:, group * N : (group + 1) * N], preferred_element_type=jnp.float32
        )


def inner_kernel(step, running, x, b, c, inner):
    heads, count = step.shape
    groups = b.shape[1] // N
    per_group = heads // groups
    total = running[...]
    columns = columns_of(total)
    line = lax.broadcasted_iota(jnp.int32, (count, count), 0)
    lane = lax.broadcasted_iota(jnp.int32, (count, count), 1)
    first = lax.broadcasted_iota(jnp.int32, (count, 2 * P_SIZE), 1) < P_SIZE
    for group in range(groups):
        where = slice(group * N, (group + 1) * N)
        scores = lax.dot_general(
            c[:, where], b[:, where], (((1,), (1,)), ((), ())), preferred_element_type=jnp.float32
        )
        scores = jnp.where(line >= lane, scores, 0.0)
        for pair in range(per_group // 2):
            head = group * per_group + 2 * pair
            mixing = []
            for h in (head, head + 1):
                spread = columns[:, h : h + 1] - total[h : h + 1]
                decay = jnp.exp(jnp.where(line >= lane, spread, 0.0))
                mixing.append((decay * scores * step[h : h + 1]).astype(jnp.bfloat16))
            both = x[:, head * P_SIZE : (head + 2) * P_SIZE].astype(jnp.float32)
            apart = jnp.concatenate(
                [jnp.where(first, both, 0.0), jnp.where(first, 0.0, both)], axis=0
            )
            inner[:, head * P_SIZE : (head + 2) * P_SIZE] = jnp.dot(
                jnp.concatenate(mixing, axis=1),
                apart.astype(jnp.bfloat16),
                preferred_element_type=jnp.float32,
            )


def project(place, rows, weight_hbm, weight, came, first, last, give):
    shares, _, width = weight.shape
    total = weight_hbm.shape[1] // width
    copies = []
    for step in range(first, last):
        start = pl.multiple_of(lax.rem(place[1] + step, total) * width, width)
        copies.append(
            pltpu.make_async_copy(
                weight_hbm.at[:, pl.ds(start, width)], weight.at[step - first], came.at[step - first]
            )
        )
    yield [copy.start() for copy in copies]
    for step in range(first, last):
        copies[step - first].wait()
        give(
            step,
            jnp.dot(rows[...], weight[step - first], preferred_element_type=jnp.float32),
        )
    yield


def own_kernel(place, normed, weight_hbm, stream, own, weight, came):
    def give(step, part):
        own[...] = part + stream[...].astype(jnp.float32)

    for _ in project(place, normed, weight_hbm, weight, came, 0, 1, give):
        pass


def mixer_kernel(place, weight_hbm, *refs):
    sources, (normed, theirs), refs = refs[:7], refs[7:9], refs[9:]
    targets, (high, low, weight, came, fetched) = refs[:7], refs[7:]
    fetches = [
        pltpu.make_async_copy(source, target, fetched.at[i])
        for i, (source, target) in enumerate(zip(sources, targets))
    ]
    for fetch in fetches:
        fetch.start()
    inner, running, c, z, mine, back, gain = targets

    def give(step, part):
        theirs[step - 1] = part.astype(jnp.bfloat16)

    projection = project(
        place, normed, weight_hbm, weight, came, 1, theirs.shape[0] + 1, give
    )
    next(projection)
    for fetch in fetches:
        fetch.wait()
    heads, count = running.shape
    groups = c.shape[1] // N
    per_group = heads // groups
    wide = per_group * P_SIZE
    half = mine.shape[0]
    odd = place[0] % 2
    for part in range(2):
        value = jnp.where(odd == part, mine[...], back[...])
        rounded = value.astype(jnp.bfloat16)
        high[part * half : (part + 1) * half] = rounded
        low[part * half : (part + 1) * half] = (value - rounded.astype(jnp.float32)).astype(
            jnp.bfloat16
        )
    growth = columns_of(jnp.exp(running[...]))
    first = lax.broadcasted_iota(jnp.int32, (count, 2 * P_SIZE), 1) < P_SIZE
    contract = (((1,), (1,)), ((), ()))
    for group in range(groups):
        where = slice(group * wide, (group + 1) * wide)
        reads = c[:, group * N : (group + 1) * N]
        carried = lax.dot_general(
            reads, high[where], contract, preferred_element_type=jnp.float32
        ) + lax.dot_general(reads, low[where], contract, preferred_element_type=jnp.float32)
        heads_in = range(group * per_group, (group + 1) * per_group, 2)
        scale = jnp.concatenate(
            [jnp.where(first, growth[:, h : h + 1], growth[:, h + 1 : h + 2]) for h in heads_in],
            axis=1,
        )
        gate = z[:, where].astype(jnp.float32)
        gated = (inner[:, where] + scale * carried) * (gate / (1.0 + jnp.exp(-gate)))
        mean = jnp.sum(gated * gated, axis=1, keepdims=True) / wide
        normed[:, where] = (gated * lax.rsqrt(mean + 1e-05) * gain[:, where]).astype(jnp.bfloat16)
    next(projection)


def per_device(
    ssm_input,
    gate_input,
    b_input,
    c_input,
    step_size,
    decay_rate,
    norm_gain,
    out_weight,
    stream,
    moe_gain,
    router,
    expert_ids,
    w_gate,
    w_up,
    w_down,
):
    token_count, inner_width = ssm_input.shape
    head_count = step_size.shape[0]
    slice_width = stream.shape[1]
    expert_count = router.shape[1]
    top_count = expert_ids.shape[1]
    exp_size = lax.axis_size("exp")
    capacity = max(
        2, token_count * top_count // expert_count + token_count * top_count // (4 * expert_count)
    )
    vmem = pl.BlockSpec(memory_space=pltpu.VMEM)
    hbm = pl.BlockSpec(memory_space=pltpu.HBM)
    state, running = pl.pallas_call(
        state_kernel,
        out_shape=[
            jax.ShapeDtypeStruct((inner_width, N), jnp.float32),
            jax.ShapeDtypeStruct(step_size.shape, jnp.float32),
        ],
        in_specs=[vmem] + [hbm] * 3,
        out_specs=[vmem] * 2,
        scratch_shapes=[
            pltpu.VMEM(step_size.shape, jnp.float32),
            pltpu.VMEM(ssm_input.shape, jnp.bfloat16),
            pltpu.VMEM(b_input.shape, jnp.bfloat16),
            pltpu.SemaphoreType.DMA((3,)),
        ],
        compiler_params=pltpu.CompilerParams(vmem_limit_bytes=16 * 2**20),
    )(decay_rate[None], step_size, ssm_input, b_input)
    id_rows = jnp.pad(expert_ids.T.astype(jnp.float32), ((0, -expert_ids.shape[1] % 8), (0, 0)))
    inner = pl.pallas_call(
        inner_kernel,
        out_shape=jax.ShapeDtypeStruct((token_count, inner_width), jnp.float32),
        in_specs=[vmem] * 5,
        out_specs=vmem,
        compiler_params=pltpu.CompilerParams(vmem_limit_bytes=16 * 2**20),
        cost_estimate=pl.CostEstimate(
            flops=4 * inner_width * token_count * token_count,
            bytes_accessed=8 * inner_width * token_count,
            transcendentals=head_count * token_count * token_count,
        ),
    )(step_size, running, ssm_input, b_input, c_input)
    here = lax.axis_index("ctx")
    place = jnp.stack([here, lax.axis_index("exp"), here ^ 1]).astype(jnp.int32)
    beside = (inner, place, norm_gain[None], moe_gain[None])
    mine, back, beside, every_ids = prefix_states(state, running[:, -1], id_rows, beside)
    inner, place, norm_row, moe_row = beside
    fetched = (
        inner,
        running,
        c_input,
        gate_input,
        mine,
        back,
        norm_row,
    )
    normed, theirs = pl.pallas_call(
        mixer_kernel,
        out_shape=[
            jax.ShapeDtypeStruct((token_count, inner_width), jnp.bfloat16),
            jax.ShapeDtypeStruct((exp_size - 1, *stream.shape), jnp.bfloat16),
        ],
        in_specs=[pl.BlockSpec(memory_space=pltpu.SMEM)] + [hbm] * 8,
        out_specs=[vmem] * 2,
        scratch_shapes=[pltpu.VMEM(array.shape, array.dtype) for array in fetched]
        + [
            pltpu.VMEM((inner_width, N), jnp.bfloat16),
            pltpu.VMEM((inner_width, N), jnp.bfloat16),
            pltpu.VMEM((exp_size - 1, inner_width, slice_width), jnp.bfloat16),
            pltpu.SemaphoreType.DMA((exp_size - 1,)),
            pltpu.SemaphoreType.DMA((7,)),
        ],
        compiler_params=pltpu.CompilerParams(vmem_limit_bytes=60 * 2**20),
    )(place, out_weight, *fetched)
    hidden_own = pl.pallas_call(
        own_kernel,
        out_shape=jax.ShapeDtypeStruct(stream.shape, jnp.float32),
        in_specs=[pl.BlockSpec(memory_space=pltpu.SMEM), vmem, hbm, vmem],
        out_specs=vmem,
        scratch_shapes=[
            pltpu.VMEM((1, inner_width, slice_width), jnp.bfloat16),
            pltpu.SemaphoreType.DMA((1,)),
        ],
        compiler_params=pltpu.CompilerParams(vmem_limit_bytes=60 * 2**20),
        cost_estimate=pl.CostEstimate(
            flops=2 * token_count * inner_width * slice_width,
            bytes_accessed=2 * inner_width * slice_width,
            transcendentals=0,
        ),
    )(place, normed, out_weight, stream)
    for step in range(1, exp_size):
        ring = [(i, (i + step) % exp_size) for i in range(exp_size)]
        sent = lax.ppermute(theirs[step - 1], "exp", ring)
        hidden_own = hidden_own + sent.astype(jnp.float32)
    hidden_own = hidden_own.astype(jnp.bfloat16)
    every_token = token_count * lax.axis_size("ctx")
    planes = lax.axis_size("ctx") // PLANE
    if exp_size == 2 and planes == 4 and every_token <= 3 * expert_count * capacity:
        return dense_experts(
            place,
            hidden_own,
            every_ids,
            top_count,
            moe_row,
            router,
            (w_gate[0], w_up[0], w_down[0]),
        )
    hidden_all = lax.all_gather(hidden_own, "exp", axis=1, tiled=True)
    hidden_f = hidden_all.astype(jnp.float32)
    mean_h = jnp.mean(hidden_f * hidden_f, axis=1, keepdims=True)
    sent_rows = (hidden_f * lax.rsqrt(mean_h + 1e-06) * moe_gain).astype(jnp.bfloat16)
    logits = jnp.dot(sent_rows, router, preferred_element_type=jnp.float32)
    sigmoid_score = jax.nn.sigmoid(logits)
    expert_range = jnp.arange(expert_count, dtype=jnp.int32)
    matches = expert_ids[:, :, None] == expert_range
    picked = jnp.sum(jnp.where(matches, sigmoid_score[:, None, :], 0.0), axis=2)
    gates = picked / jnp.sum(picked, axis=1, keepdims=True)
    flat_ids = expert_ids.reshape(-1)
    one_hot = (flat_ids[:, None] == expert_range).astype(jnp.int32)
    slot_index = jnp.sum((jnp.cumsum(one_hot, axis=0) - one_hot) * one_hot, axis=1)
    target = flat_ids * capacity + slot_index
    token_of = jnp.arange(token_count * top_count, dtype=jnp.int32) // top_count
    source_row = (
        jnp.full((expert_count * capacity,), token_count, jnp.int32).at[target].set(token_of)
    )
    padded = jnp.concatenate([sent_rows, jnp.zeros((1, sent_rows.shape[1]), jnp.bfloat16)], axis=0)
    outgoing = padded[source_row].reshape(expert_count, capacity, sent_rows.shape[1])
    returned = run_rows(
        lax.all_to_all(outgoing, "ctx", split_axis=0, concat_axis=0, tiled=True),
        w_gate,
        w_up,
        w_down,
    )
    back_width = returned.shape[2]
    flat_back = returned.reshape(expert_count * capacity, back_width)
    slot_rows = target.reshape(token_count, top_count)
    moe_part = jnp.zeros((token_count, back_width), jnp.float32)
    for choice_number in range(top_count):
        picked_rows = flat_back[slot_rows[:, choice_number]].astype(jnp.float32)
        moe_part = moe_part + gates[:, choice_number][:, None] * picked_rows
    moe_sum = lax.psum_scatter(
        moe_part.astype(jnp.bfloat16), "exp", scatter_dimension=1, tiled=True
    ).astype(jnp.float32)
    return (hidden_own.astype(jnp.float32) + moe_sum).astype(jnp.bfloat16)


def solution(mesh):
    in_specs = (
        P("ctx", "exp"),
        P("ctx", "exp"),
        P("ctx", "exp"),
        P("ctx", "exp"),
        P("exp", "ctx"),
        P("exp"),
        P("exp"),
        P("exp", None),
        P("ctx", "exp"),
        P(),
        P(),
        P("ctx", None),
        P("ctx", "exp", None),
        P("ctx", "exp", None),
        P("ctx", "exp", None),
    )
    out_specs = P("ctx", "exp")
    return jax.shard_map(
        per_device, mesh=mesh, in_specs=in_specs, out_specs=out_specs, check_vma=False
    )
```
